128 devices in a mesh: dp: 16 (over x, z), tp: 8 (over y, core).
Axes of the slice: x: 4, y: 4, z: 4, core: 2. Of those that a mesh axis runs over, the one named last changes fastest.
Arguments:
- queries: bfloat16 [256, 73728], P('dp', 'tp'), may hold values from -6 to 6
- own_latent: bfloat16 [256, 576], P('dp'), may hold values from -11 to 11
- prefix_cache: bfloat16 [2048, 36864], P(('dp', 'tp')), may hold values from -6 to 6
- block_home: int32 [2048], replicated, may hold values from 0 to 2047, as said below
- row_prompt: int32 [256], replicated, may hold values from 0 to 3, as said below
- chosen: int32 [256, 32], replicated, may hold values from 0 to 511, as said below
- value_up: bfloat16 [128, 512, 128], P('tp'), may hold values from -0.25 to 0.25
- out_weight: bfloat16 [16384, 7168], P('tp', 'dp'), may hold values from -0.046875 to 0.046875
- residual: bfloat16 [256, 7168], P(None, 'dp'), may hold values from -0.59765625 to 0.59765625
- norm_gain: bfloat16 [7168], P('dp'), may hold values from 0.099609375 to 1.8984375
- gate_weight: bfloat16 [7168, 18432], P('dp', 'tp'), may hold values from -0.0625 to 0.0625
- up_weight: bfloat16 [7168, 18432], P('dp', 'tp'), may hold values from -0.0625 to 0.0625
Outputs:
- stream: bfloat16 [256, 7168], P(None, 'dp')
- hidden: bfloat16 [256, 18432], P('dp', 'tp')
The draws below stay inside these ranges and needn't reach their ends.
Inputs may be any that keep to these rules, and one draw needn't show every extreme that they name: A permutation of the stored blocks: block b of prompt p is stored at slot block_home[p * 512 + b], and slots k * 16 to (k + 1) * 16 - 1 lie on the k-th device of dp+tp in mesh order; every device holds the same number of blocks of every prompt. `row_prompt`: the 16 rows of one dp index share one prompt; every prompt serves 4 dp indices. `chosen`: each row names 32 distinct blocks of its prompt. Together the rows of one dp index name at least one and at most 2 distinct blocks stored on any one device; in every draw some dp index names exactly 2 from every device.
All inputs are finite; a program needn't handle non-finite values.
Results may differ from the reference program's by a relative error of at most 0.04.
Values may be sent and summed in bfloat16 or wider, within the bound.
No kernel may reach another device: no remote copies, remote signals or barrier semaphores. Data moves between devices by JAX's collectives and lax.ppermute only.
A program may use at most 192 MiB of HBM per device.

```python
import math
import jax
import jax.numpy as jnp
from jax import lax

D = 7168
FF = 18432
HEADS = 128
LAT = 512
ROPE = 64
QK_NOPE = 128
VHEAD = 128
BS = 64
TOPB = 32
CAP = 2
PB = 512
R_DEV = 16
NPROMPT = 4
BLK_DEV = 16
NBLK = 2048
ROWS = 256


def layout_tables(key):
    devices = NPROMPT * PB // BLK_DEV
    per_device = PB // devices
    replicas = ROWS // R_DEV
    order_keys = jax.random.split(jax.random.fold_in(key, 101), NPROMPT)
    orders = jax.vmap(lambda subkey: jax.random.permutation(subkey, PB))(order_keys).astype(jnp.int32)
    prompt_ids = jnp.arange(NPROMPT, dtype=jnp.int32)[:, None]
    positions = jnp.broadcast_to(jnp.arange(PB, dtype=jnp.int32)[None, :], orders.shape)
    inverse = jnp.zeros_like(orders).at[prompt_ids, orders].set(positions)
    home = orders % devices * BLK_DEV + prompt_ids * per_device + orders // devices
    replica_prompt = (jax.random.permutation(jax.random.fold_in(key, 102), replicas) % NPROMPT).astype(jnp.int32)
    busiest = jax.random.randint(jax.random.fold_in(key, 103), (), 0, replicas)
    counts = jax.random.randint(jax.random.fold_in(key, 104), (replicas, devices), 1, CAP + 1)
    counts = jnp.where(jnp.arange(replicas)[:, None] == busiest, CAP, counts).astype(jnp.int32)
    pick_keys = jax.random.split(jax.random.fold_in(key, 105), replicas * devices)
    picks = jax.vmap(lambda subkey: jax.random.permutation(subkey, per_device)[:CAP])(pick_keys)
    picks = picks.reshape(replicas, devices, CAP).astype(jnp.int32)
    holder_ids = jnp.arange(devices, dtype=jnp.int32)[None, :, None]
    blocks = inverse[replica_prompt[:, None, None], holder_ids + devices * picks]
    valid = jnp.arange(CAP, dtype=jnp.int32)[None, None, :] < counts[:, :, None]
    pool = blocks.reshape(replicas, devices * CAP)
    live = valid.reshape(replicas, devices * CAP).astype(jnp.int32)
    shuffle_keys = jax.random.split(jax.random.fold_in(key, 106), replicas)
    shuffle = jax.vmap(lambda subkey: jax.random.permutation(subkey, devices * CAP))(shuffle_keys).astype(jnp.int32)
    live_shuffled = jnp.take_along_axis(live, shuffle, axis=1)
    ranking = jnp.argsort(1 - live_shuffled, axis=1, stable=True)
    arranged = jnp.take_along_axis(shuffle, ranking, axis=1)
    pool_sorted = jnp.take_along_axis(pool, arranged, axis=1)
    totals = jnp.sum(counts, axis=1)
    spots = jnp.arange(R_DEV, dtype=jnp.int32)[:, None] * TOPB + jnp.arange(TOPB, dtype=jnp.int32)[None, :]
    spots = spots.reshape(1, R_DEV * TOPB) % totals[:, None]
    chosen = jnp.take_along_axis(pool_sorted, spots, axis=1).reshape(ROWS, TOPB)
    row_prompt = jnp.repeat(replica_prompt, R_DEV)
    return (home.reshape(NBLK).astype(jnp.int32), row_prompt.astype(jnp.int32), chosen.astype(jnp.int32))


def draw_block_home(key, part):
    return layout_tables(key)[0]


def draw_row_prompt(key, part):
    return layout_tables(key)[1]


def draw_chosen(key, part):
    return layout_tables(key)[2]


def query_bases(key):
    shape = (ROWS, HEADS, LAT + ROPE)
    normal_part = jnp.clip(jax.random.normal(jax.random.fold_in(key, 201), shape, jnp.float32), -6.0, 6.0)
    return normal_part


def draw_queries(key, part):
    normal_part = query_bases(key)
    chosen_base = normal_part
    return chosen_base.reshape(ROWS, HEADS * (LAT + ROPE)).astype(jnp.bfloat16)


def draw_own_latent(key, part):
    key = jax.random.fold_in(key, 7)
    latent = jnp.clip(jax.random.normal(jax.random.fold_in(key, 1), (ROWS, LAT + ROPE), jnp.float32), -6.0, 6.0)
    return latent.astype(jnp.bfloat16)


def block_levels(rng, extent, shards, low, high):
    def one(dim, blocks):
        draws = jax.random.uniform(jax.random.fold_in(jax.random.fold_in(rng, 6), dim), (blocks,), jnp.float32, low / len(shards), high / len(shards))
        return jnp.repeat(jnp.exp(draws), extent[dim] // blocks).reshape((-1,) + (1,) * (len(extent) - dim - 1))

    gain = one(*shards[0])
    for cut in shards[1:]:
        gain = gain * one(*cut)
    return gain


def normal_values(key, extent, spread, reach, cuts=(), held_as=jnp.bfloat16):
    entries = spread * jax.random.normal(key, extent, jnp.float32)
    if cuts:
        entries = entries * block_levels(key, extent, cuts, -0.22, 0.18)
    return jnp.clip(entries, -reach, reach).astype(held_as)


def setup_inputs(seed: int = 0) -> dict:
    arg_keys = jax.random.split(jax.random.key(seed), 13)
    return {
        "queries": draw_queries(jax.random.fold_in(arg_keys[12], 71), 0),
        "own_latent": draw_own_latent(jax.random.fold_in(arg_keys[12], 71), 0),
        "prefix_cache": normal_values(arg_keys[2], (NBLK, BS * (LAT + ROPE)), 1.0, 6.0, ((0, 128),)),
        "block_home": draw_block_home(jax.random.fold_in(arg_keys[12], 71), 0),
        "row_prompt": draw_row_prompt(jax.random.fold_in(arg_keys[12], 71), 0),
        "chosen": draw_chosen(jax.random.fold_in(arg_keys[12], 71), 0),
        "value_up": normal_values(arg_keys[6], (HEADS, LAT, VHEAD), LAT ** -0.5, 0.25, ((0, 8),)),
        "out_weight": normal_values(arg_keys[7], (HEADS * VHEAD, D), (HEADS * VHEAD) ** -0.5, 0.046875, ((0, 8), (1, 16))),
        "residual": normal_values(arg_keys[8], (ROWS, D), 0.1, 0.59765625, ((1, 16),)),
        "norm_gain": jnp.clip(1.0 + 0.18 * jax.random.normal(arg_keys[9], (D,), jnp.float32), 0.099609375, 1.8984375).astype(jnp.bfloat16),
        "gate_weight": normal_values(arg_keys[10], (D, FF), D ** -0.5, 0.0625, ((0, 16), (1, 8))),
        "up_weight": normal_values(arg_keys[11], (D, FF), D ** -0.5, 0.0625, ((0, 16), (1, 8))),
    }


EPSILON = 1e-06

def reference(queries, own_latent, prefix_cache, block_home, row_prompt, chosen, value_up, out_weight, residual, norm_gain, gate_weight, up_weight):
    kv_width = LAT + ROPE
    score_scale = 1.0 / math.sqrt(QK_NOPE + ROPE)
    slot_ids = block_home[row_prompt[:, None] * PB + chosen].astype(jnp.int32)
    lift_table = value_up.astype(jnp.float32)

    def one_row(pieces):
        query_row, own_row, slot_row = pieces
        latents = jnp.take(prefix_cache, slot_row, axis=0).reshape(TOPB * BS, kv_width)
        latents = jnp.concatenate([latents, own_row[None, :]], axis=0).astype(jnp.float32)
        query_heads = query_row.reshape(HEADS, kv_width).astype(jnp.float32)
        scores = jnp.einsum('hc,nc->hn', query_heads, latents) * score_scale
        highest = lax.optimization_barrier(jnp.max(scores, axis=1, keepdims=True))
        raised = jnp.exp(scores - highest)
        weights = (raised / lax.optimization_barrier(jnp.sum(raised, axis=1, keepdims=True))).astype(jnp.bfloat16)
        mixture = jnp.einsum('hn,nc->hc', weights.astype(jnp.float32), latents[:, :LAT]).astype(jnp.bfloat16)
        lifted = jnp.einsum('hc,hcv->hv', mixture.astype(jnp.float32), lift_table).astype(jnp.bfloat16)
        return lifted.reshape(HEADS * VHEAD)
    per_head = lax.map(one_row, (queries, own_latent, slot_ids))
    attn = jnp.dot(per_head, out_weight, preferred_element_type=jnp.float32)
    stream = (residual.astype(jnp.float32) + attn).astype(jnp.bfloat16)
    stream_wide = stream.astype(jnp.float32)
    squares = lax.optimization_barrier(jnp.sum(stream_wide * stream_wide, axis=1))
    inverse = lax.rsqrt(squares / D + EPSILON)
    scaled = (stream_wide * norm_gain.astype(jnp.float32)[None, :]).astype(jnp.bfloat16)
    gate_part = jnp.dot(scaled, gate_weight, preferred_element_type=jnp.float32) * inverse[:, None]
    up_part = jnp.dot(scaled, up_weight, preferred_element_type=jnp.float32) * inverse[:, None]
    hidden = (jax.nn.silu(gate_part) * up_part).astype(jnp.bfloat16)
    return (stream, hidden)
```

```python
import math

import jax
import jax.numpy as jnp
from jax import lax
from jax.experimental import pallas as pl
from jax.experimental.pallas import tpu as pltpu
from jax.sharding import PartitionSpec as P

D = 7168
LAT = 512
ROPE = 64
QK_NOPE = 128
CAP = 2
PB = 512
BS = 64
KV = LAT + ROPE
EPSILON = 1e-06
SCALE = 1.0 / math.sqrt(QK_NOPE + ROPE)
NEG = -1e30
f32 = jnp.float32
bf16 = jnp.bfloat16


def send(x, axis, to, n):
    return lax.ppermute(x, axis, [(i, to(i)) for i in range(n)])


def swap_core(x):
    return send(x, "tp", lambda i: i ^ 1, 8)


def send_y(x, k):
    return send(x, "tp", lambda i: i ^ (2 * k), 8)


def send_x(x, k):
    return send(x, "dp", lambda i: ((i // 4 + k) % 4) * 4 + i % 4, 16)


def send_z(x, k):
    return send(x, "dp", lambda i: (i // 4) * 4 + (i % 4 + k) % 4, 16)


def fetch_kernel(picks, blocks, out, sem):
    n = out.shape[0]

    def start(i, c):
        pltpu.make_async_copy(blocks.at[picks[i]], out.at[i], sem.at[i]).start()
        return c

    def wait(i, c):
        pltpu.make_async_copy(blocks.at[picks[i]], out.at[i], sem.at[i]).wait()
        return c

    lax.fori_loop(0, n, start, 0, unroll=True)
    lax.fori_loop(0, n, wait, 0, unroll=True)


def fetch(picks, blocks):
    n = picks.shape[0]
    return pl.pallas_call(
        fetch_kernel,
        out_shape=jax.ShapeDtypeStruct((n,) + blocks.shape[1:], blocks.dtype),
        grid_spec=pltpu.PrefetchScalarGridSpec(
            num_scalar_prefetch=1,
            grid=(),
            in_specs=[pl.BlockSpec(memory_space=pl.ANY)],
            out_specs=pl.BlockSpec(memory_space=pl.ANY),
            scratch_shapes=[pltpu.SemaphoreType.DMA((n,))],
        ),
        name="fetch",
    )(picks, blocks)


def token_half(ref, half):
    n = ref.shape[0]
    parts = [
        ref[:, c * BS + half * 32 : c * BS + half * 32 + 32, :].reshape(n * 32, 128)
        for c in range(4)
    ]
    return jnp.concatenate(parts, axis=1)


def token_rope(ref, half):
    n = ref.shape[0]
    rope = ref[:, 4 * BS : 4 * BS + 32, :].reshape(n * 32, 128)
    lane = lax.broadcasted_iota(jnp.int32, rope.shape, 1)
    keep = (lane < ROPE) if half == 0 else (lane >= ROPE)
    return jnp.where(keep, rope, jnp.zeros_like(rope))


def attend_kernel(q_ref, a_ref, b_ref, bias_ref, out_ref, s_ref):
    q = q_ref[...]
    m_rows = q.shape[0]
    step = a_ref.shape[0] * 32
    top = None
    for i in range(4):
        ref, half = (a_ref, b_ref)[i // 2], i % 2
        keys = jnp.concatenate([token_half(ref, half), token_rope(ref, half)], axis=1)
        s = lax.dot_general(q, keys, (((1,), (1,)), ((), ())), preferred_element_type=f32)
        s = s.reshape(m_rows // 16, 16, step) + bias_ref[:, i * step : (i + 1) * step][None]
        s = s.reshape(m_rows, step)
        s_ref[i] = s
        high = jnp.max(s, axis=1, keepdims=True)
        top = high if top is None else jnp.maximum(top, high)
    acc = None
    total = None
    for i in range(4):
        ref, half = (a_ref, b_ref)[i // 2], i % 2
        p = jnp.exp((s_ref[i] - top) * SCALE)
        part = jnp.sum(p, axis=1, keepdims=True)
        o = jnp.dot(p.astype(bf16), token_half(ref, half), preferred_element_type=f32)
        acc = o if acc is None else acc + o
        total = part if total is None else total + part
    out_ref[:, :LAT] = (acc / total).astype(bf16)
    lse = top * SCALE + jnp.log(total)
    hi = lse.astype(bf16).astype(f32)
    mid = (lse - hi).astype(bf16).astype(f32)
    low = lse - hi - mid
    lane = lax.broadcasted_iota(jnp.int32, (m_rows, 128), 1)
    stats = jnp.where(lane == 0, hi, jnp.where(lane == 1, mid, jnp.where(lane == 2, low, 0.0)))
    out_ref[:, LAT:] = stats.astype(bf16)


def attend(q, a, b, bias):
    m_rows = q.shape[0]
    step = a.shape[0] * 32
    return pl.pallas_call(
        attend_kernel,
        out_shape=jax.ShapeDtypeStruct((m_rows, LAT + 128), bf16),
        in_specs=[pl.BlockSpec(memory_space=pltpu.VMEM)] * 4,
        out_specs=pl.BlockSpec(memory_space=pltpu.VMEM),
        scratch_shapes=[pltpu.VMEM((4, m_rows, step), f32)],
        compiler_params=pltpu.CompilerParams(vmem_limit_bytes=40 * 1024 * 1024),
        cost_estimate=pl.CostEstimate(
            flops=2 * m_rows * 4 * step * (640 + 512),
            bytes_accessed=2 * a.size * 2,
            transcendentals=m_rows * 4 * step,
        ),
        name="attend",
    )(q, a, b, bias)


def merge_kernel(o0, o1, o2, o3, q_ref, own_ref, up_ref, out_ref):
    heads, rows = 16, 16
    own = own_ref[...].astype(f32)
    q = q_ref[...].astype(f32).reshape(heads, rows, 640)
    lane = lax.broadcasted_iota(jnp.int32, (rows, 640), 1)
    key = jnp.where(lane < KV, own, 0.0)
    s_own = jnp.sum(q * key[None], axis=2, keepdims=True).reshape(heads * rows, 1) * SCALE
    lses = []
    for o in (o0, o1, o2, o3):
        lses.append(jnp.sum(o[:, LAT:].astype(f32), axis=1, keepdims=True))
    top = s_own
    for v in lses:
        top = jnp.maximum(top, v)
    e_own = jnp.exp(s_own - top)
    es = [jnp.exp(v - top) for v in lses]
    den = e_own + ((es[0] + es[1]) + (es[2] + es[3]))
    mix = (e_own / den).reshape(heads, rows, 1) * own[None, :, :LAT]
    mix = mix.reshape(heads * rows, LAT)
    for o, e in zip((o0, o1, o2, o3), es):
        mix = mix + (e / den) * o[:, :LAT].astype(f32)
    mix = mix.astype(bf16)
    for h in range(heads):
        out_ref[:, h * 128 : (h + 1) * 128] = jnp.dot(
            mix[h * rows : (h + 1) * rows], up_ref[h], preferred_element_type=f32
        ).astype(bf16)


def merge(parts, q, own, value_up):
    return pl.pallas_call(
        merge_kernel,
        out_shape=jax.ShapeDtypeStruct((16, 2048), bf16),
        in_specs=[pl.BlockSpec(memory_space=pltpu.VMEM)] * 7,
        out_specs=pl.BlockSpec(memory_space=pltpu.VMEM),
        compiler_params=pltpu.CompilerParams(vmem_limit_bytes=24 * 1024 * 1024),
        name="merge",
    )(*parts, q, own, value_up)


def local(
    queries,
    own_latent,
    prefix_cache,
    block_home,
    row_prompt,
    chosen,
    value_up,
    out_weight,
    residual,
    norm_gain,
    gate_weight,
    up_weight,
):
    replica = lax.axis_index("dp")
    lane = lax.axis_index("tp")
    me = replica * 8 + lane
    i32 = jnp.int32

    tokens = prefix_cache.reshape(16, BS, KV)
    lat = tokens[:, :, :LAT].reshape(16, BS, 4, 128).transpose(0, 2, 1, 3).reshape(16, 256, 128)
    rope = tokens[:, :, LAT:]
    rope = jnp.concatenate([rope[:, :32], rope[:, 32:]], axis=2)
    blocks = jnp.concatenate([lat, rope], axis=1)

    slots = me * 16 + jnp.arange(16, dtype=i32)
    ids = jnp.arange(2048, dtype=i32)
    held = jnp.sum(jnp.where(block_home[None, :] == slots[:, None], ids[None, :], 0), axis=1)
    wanted = (row_prompt[:, None] * PB + chosen).reshape(16, 512)
    needed = jnp.any(wanted[:, None, :] == held[None, :, None], axis=2)
    offs = jnp.arange(16, dtype=i32)
    before = jnp.sum(
        jnp.where(needed[:, None, :] & (offs[None, :] < offs[:, None])[None], 1, 0), axis=2
    )
    places = jnp.arange(CAP, dtype=i32)
    picks = jnp.sum(
        jnp.where(needed[:, None, :] & (before[:, None, :] == places[None, :, None]), offs, 0),
        axis=2,
    )

    outgoing = fetch(picks.reshape(-1), blocks).reshape(16, CAP, 288, 128)
    arrived = lax.all_to_all(outgoing, "dp", split_axis=0, concat_axis=0, tiled=True)
    mine = arrived.reshape(32, 288, 128)
    other = swap_core(mine)

    prompt = lax.dynamic_slice_in_dim(row_prompt, replica * 16, 1, 0)[0]
    home = lax.dynamic_slice_in_dim(block_home, prompt * PB, PB, 0)
    my_chosen = lax.dynamic_slice_in_dim(chosen, replica * 16, 16, 0)
    sel = jnp.any(my_chosen[:, :, None] == jnp.arange(PB, dtype=i32)[None, None, :], axis=1)
    need = jnp.any(sel, axis=0)
    holder = home // 16
    rank = jnp.sum(
        jnp.where(
            need[None, :] & (holder[None, :] == holder[:, None]) & (home[None, :] < home[:, None]),
            1,
            0,
        ),
        axis=1,
    )
    j = jnp.arange(32, dtype=i32)
    dev = jnp.concatenate([(j // 2) * 8 + lane, (j // 2) * 8 + (lane ^ 1)])
    place = jnp.concatenate([j % 2, j % 2])
    key = jnp.where(need, holder * 2 + rank, -1)
    hit = key[:, None] == (dev * 2 + place)[None, :]
    use = jnp.dot(sel.astype(bf16), hit.astype(bf16), preferred_element_type=f32)
    bias = jnp.where(use > 0.5, 0.0, NEG).reshape(16, 2, 1, 32, 1)
    bias = jnp.broadcast_to(bias, (16, 2, 2, 32, 32)).reshape(16, 4096)

    q = queries.reshape(16, 16, KV).transpose(1, 0, 2).reshape(256, KV)
    q = jnp.concatenate([q, q[:, LAT:]], axis=1)
    own = jnp.concatenate([own_latent, own_latent[:, LAT:]], axis=1)
    q_from = {k: send_y(q, k) for k in (2, 1, 3)}
    parts = []
    for k in (2, 1, 3):
        parts.append(send_y(attend(q_from[k], mine, other, bias), k))
    parts.append(attend(q, mine, other, bias))
    per_head = merge(parts, q, own, value_up)

    gx = jnp.concatenate([per_head] + [send_x(per_head, 4 - k) for k in (1, 2, 3)], axis=0)
    gz = jnp.concatenate([gx] + [send_z(gx, 4 - k) for k in (1, 2, 3)], axis=0)
    partial_attn = jnp.dot(gz, out_weight, preferred_element_type=f32)

    px, pz = replica // 4, replica % 4
    res = residual.reshape(4, 4, 16, 448)
    res = jnp.concatenate([res, res], axis=0)
    res = lax.dynamic_slice_in_dim(res, px, 4, 0)
    res = jnp.concatenate([res, res], axis=1)
    res = lax.dynamic_slice_in_dim(res, pz, 4, 1)
    res = res.transpose(1, 0, 2, 3).reshape(256, 448)

    core = lane % 2
    keep = lax.dynamic_slice_in_dim(partial_attn, core * 128, 128, 0)
    give = lax.dynamic_slice_in_dim(partial_attn, (1 - core) * 128, 128, 0)
    pair = (keep + swap_core(give.astype(bf16)).astype(f32)).astype(bf16)
    t1, t2, t3 = (send_y(pair, k).astype(f32) for k in (1, 2, 3))
    attn = (pair.astype(f32) + t1) + (t2 + t3)
    half = (lax.dynamic_slice_in_dim(res, core * 128, 128, 0).astype(f32) + attn).astype(bf16)
    half_other = swap_core(half)
    first = jnp.where(core == 0, half, half_other)
    second = jnp.where(core == 0, half_other, half)
    stream = jnp.concatenate([first, second], axis=0)

    wide = stream.astype(f32)
    squares = jnp.sum(wide * wide, axis=1)
    hi = lax.reduce_precision(squares, 8, 7)
    low = squares - hi
    col = lax.broadcasted_iota(i32, (256, 128), 1)
    tail = jnp.where(
        col == 0, hi[:, None], jnp.where(col == 1, low[:, None], 0.0)
    ).astype(bf16)
    scaled = (wide * norm_gain.astype(f32)[None, :]).astype(bf16)
    gate = jnp.dot(scaled, gate_weight, preferred_element_type=f32).astype(bf16)
    up = jnp.dot(scaled, up_weight, preferred_element_type=f32).astype(bf16)
    gate = jnp.concatenate([gate, tail], axis=1).reshape(4, 4, 16, 2304 + 128)
    up = up.reshape(4, 4, 16, 2304)

    g_in = [send_x(gate[:, k], k) for k in (2, 1, 3)]
    u_in = [send_z(up[k], k) for k in (2, 1, 3)]

    def add(own_part, got):
        return (own_part.astype(f32) + got[0].astype(f32)) + (
            got[1].astype(f32) + got[2].astype(f32)
        )

    g1 = add(gate[:, 0], g_in)
    u1 = add(up[0], u_in).astype(bf16)
    sq1 = g1[:, :, 2304:2305] + g1[:, :, 2305:2306]
    hi1 = lax.reduce_precision(sq1, 8, 7)
    col1 = lax.broadcasted_iota(i32, (4, 16, 128), 2)
    tail1 = jnp.where(col1 == 0, hi1, jnp.where(col1 == 1, sq1 - hi1, 0.0))
    g1 = jnp.concatenate([g1[:, :, :2304], tail1], axis=2).astype(bf16)
    g_in = [send_z(g1[k], k) for k in (2, 1, 3)]
    u_in = [send_x(u1[k], k) for k in (2, 1, 3)]
    g2 = add(g1[0], g_in)
    u2 = add(u1[0], u_in)
    sq = g2[:, 2304:2305] + g2[:, 2305:2306]
    inverse = lax.rsqrt(sq / D + EPSILON)
    gate_part = g2[:, :2304] * inverse
    up_part = u2 * inverse
    hidden = (jax.nn.silu(gate_part) * up_part).astype(bf16)

    out = stream.reshape(4, 4, 16, 448)
    out = jnp.concatenate([out, out], axis=0)
    out = lax.dynamic_slice_in_dim(out, 4 - pz, 4, 0)
    out = jnp.concatenate([out, out], axis=1)
    out = lax.dynamic_slice_in_dim(out, 4 - px, 4, 1)
    out = out.transpose(1, 0, 2, 3).reshape(256, 448)
    return (out, hidden)


def solution(mesh):
    placed = (
        P("dp", "tp"),
        P("dp", None),
        P(("dp", "tp"), None),
        P(),
        P(),
        P(),
        P("tp", None, None),
        P("tp", "dp"),
        P(None, "dp"),
        P("dp"),
        P("dp", "tp"),
        P("dp", "tp"),
    )
    return jax.shard_map(
        local, mesh=mesh, in_specs=placed, out_specs=(P(None, "dp"), P("dp", "tp")), check_vma=False
    )
```

```python
import functools
import math

import jax
import jax.numpy as jnp
from jax import lax
from jax.experimental import pallas as pl
from jax.experimental.pallas import tpu as pltpu
from jax.sharding import PartitionSpec as P

D = 7168
LAT = 512
ROPE = 64
QK_NOPE = 128
CAP = 2
PB = 512
BS = 64
KV = LAT + ROPE
EPSILON = 1e-06
SCALE = 1.0 / math.sqrt(QK_NOPE + ROPE)
SCALE2 = SCALE / math.log(2.0)
NEG = -1e30
f32 = jnp.float32
bf16 = jnp.bfloat16


def send(x, axis, to, n):
    return lax.ppermute(x, axis, [(i, to(i)) for i in range(n)])


def swap_core(x):
    return send(x, "tp", lambda i: i ^ 1, 8)


def send_y(x, k):
    return send(x, "tp", lambda i: i ^ (2 * k), 8)


def send_x(x, k):
    return send(x, "dp", lambda i: ((i // 4 + k) % 4) * 4 + i % 4, 16)


def send_z(x, k):
    return send(x, "dp", lambda i: (i // 4) * 4 + (i % 4 + k) % 4, 16)


def fetch_kernel(picks, tokens, *outs):
    px, pz = picks[32] // 4, picks[32] % 4
    for place in range(CAP):
        for first in range(4):
            for second in range(4):
                kx, kz = (first, second) if place == 0 else (second, first)
                dest = ((px + kx) % 4) * 4 + (pz + kz) % 4
                pick = picks[dest * CAP + place]
                out = outs[place * 4 + first]
                for c in range(4):
                    out[second, c * BS : (c + 1) * BS, :] = tokens[pick, :, c * 128 : (c + 1) * 128]
                rope = tokens[pick, :, LAT:KV]
                out[second, 4 * BS :, :] = jnp.concatenate([rope[:32], rope[32:]], axis=1)


def fetch(picks, tokens):
    return pl.pallas_call(
        fetch_kernel,
        out_shape=[jax.ShapeDtypeStruct((4, 288, 128), bf16)] * 8,
        grid_spec=pltpu.PrefetchScalarGridSpec(
            num_scalar_prefetch=1,
            grid=(),
            in_specs=[pl.BlockSpec(memory_space=pltpu.VMEM)],
            out_specs=[pl.BlockSpec(memory_space=pltpu.VMEM)] * 8,
        ),
        compiler_params=pltpu.CompilerParams(vmem_limit_bytes=16 * 1024 * 1024),
        name="fetch",
    )(picks, tokens)


def half_latent(refs, half):
    rows = []
    for ref in refs:
        parts = [
            ref[:, c * BS + half * 32 : c * BS + half * 32 + 32, :].reshape(-1, 128)
            for c in range(4)
        ]
        rows.append(jnp.concatenate(parts, axis=1))
    return jnp.concatenate(rows, axis=0)


def half_rope(refs, half):
    rope = jnp.concatenate(
        [ref[:, 4 * BS : 4 * BS + 32, :].reshape(-1, 128) for ref in refs], axis=0
    )
    lane = lax.broadcasted_iota(jnp.int32, rope.shape, 1)
    keep = (lane < ROPE) if half == 0 else (lane >= ROPE)
    return jnp.where(keep, rope, jnp.zeros_like(rope))


def attend_kernel(groups, resume, last, *refs):
    q_ref, bias_ref = refs[0], refs[1]
    pieces = refs[2 : 2 + 4 * groups]
    refs = refs[2 + 4 * groups :]
    if resume:
        acc_in, stat_in = refs[0], refs[1]
        refs = refs[2:]
    q = q_ref[...]
    m_rows = q.shape[0]

    def values(g):
        mine = pieces[4 * g : 4 * g + 4]
        return jnp.concatenate([half_latent(mine, 0), half_latent(mine, 1)], axis=0)

    def scores(g):
        mine = pieces[4 * g : 4 * g + 4]
        ropes = jnp.concatenate([half_rope(mine, 0), half_rope(mine, 1)], axis=0)
        keys = jnp.concatenate([values(g), ropes], axis=1)
        s = lax.dot_general(q, keys, (((1,), (1,)), ((), ())), preferred_element_type=f32)
        n = s.shape[1]
        s = s.reshape(m_rows // 16, 16, n) + bias_ref[:, g * n : (g + 1) * n][None]
        return s.reshape(m_rows, n)

    top = total = acc = None
    if resume:
        top, total, acc = stat_in[:, 0:1], stat_in[:, 64:65], acc_in[...]
    s = scores(0)
    for g in range(groups):
        ahead = scores(g + 1) if g + 1 < groups else None
        high = jnp.max(s, axis=1, keepdims=True)
        new = high if top is None else jnp.maximum(top, high)
        p = jnp.exp2((s - new) * SCALE2)
        part = jnp.sum(p, axis=1, keepdims=True)
        o = jnp.dot(p.astype(bf16), values(g), preferred_element_type=f32)
        if top is None:
            acc, total = o, part
        else:
            fade = jnp.exp2((top - new) * SCALE2)
            acc, total = acc * fade + o, total * fade + part
        top, s = new, ahead
    lane = lax.broadcasted_iota(jnp.int32, (m_rows, 128), 1)
    if not last:
        refs[0][...] = acc
        refs[1][...] = jnp.where(lane < 64, top, total)
        return
    out_ref = refs[0]
    out_ref[:, :LAT] = (acc / total).astype(bf16)
    lse = top * SCALE + jnp.log(total)
    hi = lse.astype(bf16).astype(f32)
    mid = (lse - hi).astype(bf16).astype(f32)
    low = lse - hi - mid
    stats = jnp.where(lane == 0, hi, jnp.where(lane == 1, mid, jnp.where(lane == 2, low, 0.0)))
    out_ref[:, LAT:] = stats.astype(bf16)


def attend(q, bias, pieces, carry=(), last=True):
    m_rows = q.shape[0]
    groups = len(pieces) // 4
    if last:
        shape = jax.ShapeDtypeStruct((m_rows, LAT + 128), bf16)
    else:
        shape = [
            jax.ShapeDtypeStruct((m_rows, LAT), f32),
            jax.ShapeDtypeStruct((m_rows, 128), f32),
        ]
    vmem = pl.BlockSpec(memory_space=pltpu.VMEM)
    return pl.pallas_call(
        functools.partial(attend_kernel, groups, bool(carry), last),
        out_shape=shape,
        in_specs=[vmem] * (2 + len(pieces) + len(carry)),
        out_specs=vmem if last else [vmem] * 2,
        compiler_params=pltpu.CompilerParams(vmem_limit_bytes=20 * 1024 * 1024),
        cost_estimate=pl.CostEstimate(
            flops=2 * m_rows * groups * 1024 * (768 + 512) * 2,
            bytes_accessed=groups * 4 * 4 * 288 * 128 * 2,
            transcendentals=m_rows * groups * 1024,
        ),
        name="attend",
    )(q, bias, *pieces, *carry)


def merge_kernel(o0, o1, o2, o3, q_ref, own_ref, up_ref, out_ref):
    heads, rows = 16, 16
    own = own_ref[...].astype(f32)
    q = q_ref[...].astype(f32).reshape(heads, rows, 640)
    lane = lax.broadcasted_iota(jnp.int32, (rows, 640), 1)
    key = jnp.where(lane < KV, own, 0.0)
    s_own = jnp.sum(q * key[None], axis=2, keepdims=True).reshape(heads * rows, 1) * SCALE
    lses = []
    for o in (o0, o1, o2, o3):
        lses.append(jnp.sum(o[:, LAT:].astype(f32), axis=1, keepdims=True))
    top = s_own
    for v in lses:
        top = jnp.maximum(top, v)
    e_own = jnp.exp(s_own - top)
    es = [jnp.exp(v - top) for v in lses]
    den = e_own + ((es[0] + es[1]) + (es[2] + es[3]))
    mix = (e_own / den).reshape(heads, rows, 1) * own[None, :, :LAT]
    mix = mix.reshape(heads * rows, LAT)
    for o, e in zip((o0, o1, o2, o3), es):
        mix = mix + (e / den) * o[:, :LAT].astype(f32)
    mix = mix.astype(bf16)
    for h in range(heads):
        out_ref[:, h * 128 : (h + 1) * 128] = jnp.dot(
            mix[h * rows : (h + 1) * rows], up_ref[h], preferred_element_type=f32
        ).astype(bf16)


def merge(parts, q, own, value_up):
    return pl.pallas_call(
        merge_kernel,
        out_shape=jax.ShapeDtypeStruct((16, 2048), bf16),
        in_specs=[pl.BlockSpec(memory_space=pltpu.VMEM)] * 7,
        out_specs=pl.BlockSpec(memory_space=pltpu.VMEM),
        compiler_params=pltpu.CompilerParams(vmem_limit_bytes=24 * 1024 * 1024),
        name="merge",
    )(*parts, q, own, value_up)


def ffn_kernel(core_ref, half_ref, other_ref, gain_ref, wg_ref, wu_ref, stream_ref, *outs):
    core = core_ref[0]
    half, other = half_ref[...].astype(f32), other_ref[...].astype(f32)
    wide = jnp.concatenate(
        [jnp.where(core == 0, half, other), jnp.where(core == 0, other, half)], axis=0
    )
    stream_ref[...] = wide.astype(bf16)
    squares = jnp.sum(wide * wide, axis=1, keepdims=True)
    hi = squares.astype(bf16).astype(f32)
    lane = lax.broadcasted_iota(jnp.int32, (256, 128), 1)
    tail = jnp.where(lane == 0, hi, jnp.where(lane == 1, squares - hi, 0.0)).astype(bf16)
    scaled = (wide * gain_ref[...].astype(f32)).astype(bf16)
    gate = jnp.dot(scaled, wg_ref[...], preferred_element_type=f32).astype(bf16)
    gate = gate.reshape(4, 4, 16, 2304)
    tail = tail.reshape(4, 4, 16, 128)
    for k in range(4):
        outs[k][:, :, :2304] = gate[:, k]
        outs[k][:, :, 2304:] = tail[:, k]
    up = jnp.dot(scaled, wu_ref[...], preferred_element_type=f32).astype(bf16)
    up = up.reshape(4, 4, 16, 2304)
    for k in range(4):
        outs[4 + k][...] = up[k]


def ffn(core, half, other, gain, wg, wu):
    vmem = pl.BlockSpec(memory_space=pltpu.VMEM)
    return pl.pallas_call(
        ffn_kernel,
        out_shape=[jax.ShapeDtypeStruct((256, 448), bf16)]
        + [jax.ShapeDtypeStruct((4, 16, 2304 + 128), bf16)] * 4
        + [jax.ShapeDtypeStruct((4, 16, 2304), bf16)] * 4,
        in_specs=[pl.BlockSpec(memory_space=pltpu.SMEM)] + [vmem] * 5,
        out_specs=[vmem] * 9,
        compiler_params=pltpu.CompilerParams(vmem_limit_bytes=24 * 1024 * 1024),
        name="ffn",
    )(core, half, other, gain, wg, wu)


def add4(a, b, c, d):
    return (a.astype(f32) + b.astype(f32)) + (c.astype(f32) + d.astype(f32))


def local(
    queries,
    own_latent,
    prefix_cache,
    block_home,
    row_prompt,
    chosen,
    value_up,
    out_weight,
    residual,
    norm_gain,
    gate_weight,
    up_weight,
):
    replica = lax.axis_index("dp")
    lane = lax.axis_index("tp")
    px, pz = replica // 4, replica % 4
    core = lane % 2
    me = replica * 8 + lane
    i32 = jnp.int32

    q = queries.reshape(16, 16, KV).transpose(1, 0, 2).reshape(256, KV)
    q = jnp.concatenate([q, q[:, LAT:]], axis=1)
    own = jnp.concatenate([own_latent, own_latent[:, LAT:]], axis=1)
    q_from = {k: send_y(q, k) for k in (2, 1, 3)}
    q_from[0] = q

    slots = me * 16 + jnp.arange(16, dtype=i32)
    ids = jnp.arange(2048, dtype=i32)
    held = jnp.sum(jnp.where(block_home[None, :] == slots[:, None], ids[None, :], 0), axis=1)
    wanted = (row_prompt[:, None] * PB + chosen).reshape(16, 512)
    needed = jnp.any(wanted[:, None, :] == held[None, :, None], axis=2)
    offs = jnp.arange(16, dtype=i32)
    before = jnp.sum(
        jnp.where(needed[:, None, :] & (offs[None, :] < offs[:, None])[None], 1, 0), axis=2
    )
    places = jnp.arange(CAP, dtype=i32)
    picks = jnp.sum(
        jnp.where(needed[:, None, :] & (before[:, None, :] == places[None, :, None]), offs, 0),
        axis=2,
    )
    picks = jnp.concatenate([picks.reshape(-1), replica.reshape(1)])

    sent = fetch(picks, prefix_cache.reshape(16, BS, KV))
    a_got = [sent[0]] + [None] * 3
    b_got = [sent[4]] + [None] * 3
    for k in (2, 1, 3):
        a_got[k] = send_x(sent[k], k)
        b_got[k] = send_z(sent[4 + k], k)
    a_next = jnp.stack(a_got, axis=1)
    b_next = jnp.stack(b_got, axis=1)
    a_in = [a_next[0]] + [None] * 3
    b_in = [b_next[0]] + [None] * 3
    for k in (2, 1, 3):
        a_in[k] = send_z(a_next[k], k)
        b_in[k] = send_x(b_next[k], k)
    pieces = []
    for k in (0, 2, 1, 3):
        pieces += [a_in[k], b_in[k], swap_core(a_in[k]), swap_core(b_in[k])]

    prompt = lax.dynamic_slice_in_dim(row_prompt, replica * 16, 1, 0)[0]
    home = lax.dynamic_slice_in_dim(block_home, prompt * PB, PB, 0)
    my_chosen = lax.dynamic_slice_in_dim(chosen, replica * 16, 16, 0)
    sel = jnp.any(my_chosen[:, :, None] == jnp.arange(PB, dtype=i32)[None, None, :], axis=1)
    need = jnp.any(sel, axis=0)
    holder = home // 16
    rank = jnp.sum(
        jnp.where(
            need[None, :] & (holder[None, :] == holder[:, None]) & (home[None, :] < home[:, None]),
            1,
            0,
        ),
        axis=1,
    )
    g = jnp.array([0, 2, 1, 3], i32)[:, None, None, None]
    sib = jnp.array([0, 1], i32)[None, :, None, None]
    place = jnp.array([0, 1], i32)[None, None, :, None]
    j = jnp.arange(4, dtype=i32)[None, None, None, :]
    kx = jnp.where(place == 0, j, g)
    kz = jnp.where(place == 0, g, j)
    dev = (((px - kx) % 4) * 4 + (pz - kz) % 4) * 8 + (lane ^ sib)
    want_key = (dev * 2 + place).reshape(64)
    key = jnp.where(need, holder * 2 + rank, -1)
    hit = key[:, None] == want_key[None, :]
    use = jnp.dot(sel.astype(bf16), hit.astype(bf16), preferred_element_type=f32)
    bias = jnp.where(use > 0.5, 0.0, NEG).reshape(16, 4, 1, 16, 1)
    bias = jnp.broadcast_to(bias, (16, 4, 2, 16, 32)).reshape(16, 4096)

    parts = [send_y(attend(q_from[k], bias, pieces), k) for k in (2, 1, 3)]
    parts.append(attend(q, bias, pieces))
    per_head = merge(parts, q, own, value_up)

    gx = jnp.concatenate([per_head] + [send_x(per_head, 4 - k) for k in (1, 2, 3)], axis=0)
    gz = jnp.concatenate([gx] + [send_z(gx, 4 - k) for k in (1, 2, 3)], axis=0)
    partial_attn = jnp.dot(gz, out_weight, preferred_element_type=f32)

    res = residual.reshape(4, 4, 16, 448)
    res = jnp.concatenate([res, res], axis=0)
    res = lax.dynamic_slice_in_dim(res, px, 4, 0)
    res = jnp.concatenate([res, res], axis=1)
    res = lax.dynamic_slice_in_dim(res, pz, 4, 1)
    res = res.transpose(1, 0, 2, 3).reshape(256, 448)
    res = lax.dynamic_slice_in_dim(res, core * 128, 128, 0)

    keep = lax.dynamic_slice_in_dim(partial_attn, core * 128, 128, 0)
    give = lax.dynamic_slice_in_dim(partial_attn, (1 - core) * 128, 128, 0)
    pair = (keep + swap_core(give.astype(bf16)).astype(f32)).astype(bf16)
    t = [send_y(pair, k) for k in (1, 2, 3)]
    half = (res.astype(f32) + add4(pair, *t)).astype(bf16)
    half_other = swap_core(half)
    stream, *terms = ffn(
        core.reshape(1), half, half_other, norm_gain.reshape(1, 448), gate_weight, up_weight
    )

    g_in = [send_x(terms[k], k) for k in (2, 1, 3)]
    u_in = [send_z(terms[4 + k], k) for k in (2, 1, 3)]
    g1 = add4(terms[0], *g_in)
    u1 = add4(terms[4], *u_in).astype(bf16)
    sq1 = g1[:, :, 2304:2305] + g1[:, :, 2305:2306]
    hi1 = lax.reduce_precision(sq1, 8, 7)
    col1 = lax.broadcasted_iota(i32, (4, 16, 128), 2)
    tail1 = jnp.where(col1 == 0, hi1, jnp.where(col1 == 1, sq1 - hi1, 0.0))
    g1 = jnp.concatenate([g1[:, :, :2304], tail1], axis=2).astype(bf16)
    stream, g1 = lax.optimization_barrier((stream, g1))
    g_in = [send_z(g1[k], k) for k in (2, 1, 3)]
    u_in = [send_x(u1[k], k) for k in (2, 1, 3)]
    g2 = add4(g1[0], *g_in)
    u2 = add4(u1[0], *u_in)
    sq = g2[:, 2304:2305] + g2[:, 2305:2306]
    inverse = lax.rsqrt(sq / D + EPSILON)
    gate_part = g2[:, :2304] * inverse
    up_part = u2 * inverse
    hidden = (jax.nn.silu(gate_part) * up_part).astype(bf16)

    out = stream.reshape(4, 4, 16, 448)
    out = jnp.concatenate([out, out], axis=0)
    out = lax.dynamic_slice_in_dim(out, 4 - pz, 4, 0)
    out = jnp.concatenate([out, out], axis=1)
    out = lax.dynamic_slice_in_dim(out, 4 - px, 4, 1)
    out = out.transpose(1, 0, 2, 3).reshape(256, 448)
    return (out, hidden)


def solution(mesh):
    placed = (
        P("dp", "tp"),
        P("dp", None),
        P(("dp", "tp"), None),
        P(),
        P(),
        P(),
        P("tp", None, None),
        P("tp", "dp"),
        P(None, "dp"),
        P("dp"),
        P("dp", "tp"),
        P("dp", "tp"),
    )
    return jax.shard_map(
        local, mesh=mesh, in_specs=placed, out_specs=(P(None, "dp"), P("dp", "tp")), check_vma=False
    )
```

```python
import functools
import math

import jax
import jax.numpy as jnp
from jax import lax
from jax.experimental import pallas as pl
from jax.experimental.pallas import tpu as pltpu
from jax.sharding import PartitionSpec as P

D = 7168
LAT = 512
ROPE = 64
QK_NOPE = 128
CAP = 2
PB = 512
BS = 64
KV = LAT + ROPE
EPSILON = 1e-06
FF = 2304
SCALE = 1.0 / math.sqrt(QK_NOPE + ROPE)
SCALE2 = SCALE / math.log(2.0)
NEG = -1e30
f32 = jnp.float32
bf16 = jnp.bfloat16


def send(x, axis, to, n):
    return lax.ppermute(x, axis, [(i, to(i)) for i in range(n)])


def swap_core(x):
    return send(x, "tp", lambda i: i ^ 1, 8)


def send_y(x, k):
    return send(x, "tp", lambda i: i ^ (2 * k), 8)


def send_dp(x, stage, k):
    pairs = []
    for i in range(128):
        dp, tp = i // 8, i % 8
        if tp % 2 == stage:
            to = ((dp // 4 + k) % 4) * 4 + dp % 4
        else:
            to = (dp // 4) * 4 + (dp % 4 + k) % 4
        pairs.append((i, to * 8 + tp))
    return lax.ppermute(x, ("dp", "tp"), pairs)


VMEM = pl.BlockSpec(memory_space=pltpu.VMEM)
SMEM = pl.BlockSpec(memory_space=pltpu.SMEM)


def call(kernel, name, outs, ins, scalars=0, limit=20, **kw):
    return pl.pallas_call(
        kernel,
        out_shape=outs,
        in_specs=[SMEM] * scalars + [VMEM] * (len(ins) - scalars),
        out_specs=[VMEM] * len(outs),
        compiler_params=pltpu.CompilerParams(vmem_limit_bytes=limit * 1024 * 1024),
        name=name,
        **kw,
    )(*ins)


def shape(*dims, dtype=bf16):
    return jax.ShapeDtypeStruct(dims, dtype)


def place_of(where, ka, kb):
    px, pz, core = where[0], where[1], where[2]
    kx = jnp.where(core == 0, ka, kb)
    kz = jnp.where(core == 0, kb, ka)
    return ((px + kx) % 4) * 4 + (pz + kz) % 4


def fetch_kernel(where, picks, tokens, *outs):
    for ka in range(4):
        for kb in range(4):
            dest = place_of(where, ka, kb)
            for rank in range(CAP):
                pick = picks[dest * CAP + rank]
                out = outs[ka]
                at = kb * CAP + rank
                for c in range(4):
                    out[at, c * BS : (c + 1) * BS, :] = tokens[pick, :, c * 128 : (c + 1) * 128]
                rope = tokens[pick, :, LAT:KV]
                out[at, 4 * BS :, :] = jnp.concatenate([rope[:32], rope[32:]], axis=1)


def regroup_kernel(*refs):
    for ka in range(4):
        for kb in range(4):
            refs[4 + kb][ka * CAP : (ka + 1) * CAP] = refs[ka][kb * CAP : (kb + 1) * CAP]


def half_latent(refs, half):
    rows = []
    for ref in refs:
        parts = [
            ref[:, c * BS + half * 32 : c * BS + half * 32 + 32, :].reshape(-1, 128)
            for c in range(4)
        ]
        rows.append(jnp.concatenate(parts, axis=1))
    return jnp.concatenate(rows, axis=0)


def half_rope(refs, half):
    rope = jnp.concatenate(
        [ref[:, 4 * BS : 4 * BS + 32, :].reshape(-1, 128) for ref in refs], axis=0
    )
    lane = lax.broadcasted_iota(jnp.int32, rope.shape, 1)
    keep = (lane < ROPE) if half == 0 else (lane >= ROPE)
    return jnp.where(keep, rope, jnp.zeros_like(rope))


def attend_kernel(groups, resume, last, *refs):
    index, q_ref, bias_ref = refs[:3]
    pieces = refs[3 : 3 + 2 * groups]
    refs = refs[3 + 2 * groups :]
    if resume:
        acc_in, stat_in = refs[0], refs[1]
        refs = refs[2:]
    q = q_ref[index[0]]
    m_rows = q.shape[0]

    def values(g):
        mine = pieces[2 * g : 2 * g + 2]
        return jnp.concatenate([half_latent(mine, 0), half_latent(mine, 1)], axis=0)

    def scores(g):
        mine = pieces[2 * g : 2 * g + 2]
        ropes = jnp.concatenate([half_rope(mine, 0), half_rope(mine, 1)], axis=0)
        keys = jnp.concatenate([values(g), ropes], axis=1)
        s = lax.dot_general(q, keys, (((1,), (1,)), ((), ())), preferred_element_type=f32)
        n = s.shape[1]
        s = s.reshape(m_rows // 16, 16, n) + bias_ref[:, g * n : (g + 1) * n][None]
        return s.reshape(m_rows, n)

    top = total = acc = None
    if resume:
        top, total, acc = stat_in[:, 0:1], stat_in[:, 64:65], acc_in[...]
    s = scores(0)
    for g in range(groups):
        ahead = scores(g + 1) if g + 1 < groups else None
        high = jnp.max(s, axis=1, keepdims=True)
        new = high if top is None else jnp.maximum(top, high)
        p = jnp.exp2((s - new) * SCALE2)
        part = jnp.sum(p, axis=1, keepdims=True)
        o = jnp.dot(p.astype(bf16), values(g), preferred_element_type=f32)
        if top is None:
            acc, total = o, part
        else:
            fade = jnp.exp2((top - new) * SCALE2)
            acc, total = acc * fade + o, total * fade + part
        top, s = new, ahead
    lane = lax.broadcasted_iota(jnp.int32, (m_rows, 128), 1)
    if not last:
        refs[0][...] = acc
        refs[1][...] = jnp.where(lane < 64, top, total)
        return
    out_ref = refs[0]
    out_ref[:, :LAT] = (acc / total).astype(bf16)
    lse = top * SCALE + jnp.log(total)
    hi = lse.astype(bf16).astype(f32)
    mid = (lse - hi).astype(bf16).astype(f32)
    low = lse - hi - mid
    stats = jnp.where(lane == 0, hi, jnp.where(lane == 1, mid, jnp.where(lane == 2, low, 0.0)))
    out_ref[:, LAT:] = stats.astype(bf16)


def attend(index, q, bias, pieces, carry=(), last=True):
    m_rows = q.shape[1]
    groups = len(pieces) // 2
    if last:
        outs = [shape(m_rows, LAT + 128)]
    else:
        outs = [shape(m_rows, LAT, dtype=f32), shape(m_rows, 128, dtype=f32)]
    cost = pl.CostEstimate(
        flops=2 * m_rows * groups * 1024 * (768 + 512) * 2,
        bytes_accessed=groups * 16 * 288 * 128 * 2,
        transcendentals=m_rows * groups * 1024,
    )
    return call(
        functools.partial(attend_kernel, groups, bool(carry), last),
        "attend",
        outs,
        [index, q, bias, *pieces, *carry],
        scalars=1,
        cost_estimate=cost,
    )


def merge_kernel(o0, o1, o2, o3, q_ref, own_ref, up_ref, out_ref):
    heads, rows = 16, 16
    own = own_ref[...].astype(f32)
    q = q_ref[...].astype(f32).reshape(heads, rows, 640)
    lane = lax.broadcasted_iota(jnp.int32, (rows, 640), 1)
    key = jnp.where(lane < KV, own, 0.0)
    s_own = jnp.sum(q * key[None], axis=2, keepdims=True).reshape(heads * rows, 1) * SCALE
    lses = []
    for o in (o0, o1, o2, o3):
        lses.append(jnp.sum(o[:, LAT:].astype(f32), axis=1, keepdims=True))
    top = s_own
    for v in lses:
        top = jnp.maximum(top, v)
    e_own = jnp.exp(s_own - top)
    es = [jnp.exp(v - top) for v in lses]
    den = e_own + ((es[0] + es[1]) + (es[2] + es[3]))
    mix = (e_own / den).reshape(heads, rows, 1) * own[None, :, :LAT]
    mix = mix.reshape(heads * rows, LAT)
    for o, e in zip((o0, o1, o2, o3), es):
        mix = mix + (e / den) * o[:, :LAT].astype(f32)
    mix = mix.astype(bf16)
    for h in range(heads):
        out_ref[:, h * 128 : (h + 1) * 128] = jnp.dot(
            mix[h * rows : (h + 1) * rows], up_ref[h], preferred_element_type=f32
        ).astype(bf16)


def merge(parts, q, own, value_up):
    return pl.pallas_call(
        merge_kernel,
        out_shape=jax.ShapeDtypeStruct((16, 2048), bf16),
        in_specs=[pl.BlockSpec(memory_space=pltpu.VMEM)] * 7,
        out_specs=pl.BlockSpec(memory_space=pltpu.VMEM),
        compiler_params=pltpu.CompilerParams(vmem_limit_bytes=24 * 1024 * 1024),
        name="merge",
    )(*parts, q, own, value_up)


def project_kernel(where, p0, p1, p2, p3, weight, keep_ref, give_ref):
    core = where[2]
    rows = jnp.concatenate([p0[...], p1[...], p2[...], p3[...]], axis=0)
    full = lax.dot_general(
        rows, weight[...], (((1,), (1,)), ((), ())), preferred_element_type=f32
    ).reshape(4, 4, 16, 448)

    @pl.when(core == 0)
    def _():
        keep_ref[...] = full[:2]
        give_ref[...] = full[2:].astype(bf16)

    @pl.when(core == 1)
    def _():
        for i in range(2):
            keep_ref[i] = full[:, 2 + i]
            give_ref[i] = full[:, i].astype(bf16)


def join_kernel(where, pair, t1, t2, t3, residual, out):
    px, pz, core = where[0], where[1], where[2]
    for i in range(2):
        for kx in range(4):
            kz = core * 2 + i
            dp = ((px + kx) % 4) * 4 + (pz + kz) % 4
            attn = (pair[i, kx].astype(f32) + t1[i, kx].astype(f32)) + (
                t2[i, kx].astype(f32) + t3[i, kx].astype(f32)
            )
            out[i, kx] = (residual[dp].astype(f32) + attn).astype(bf16)


def ffn_kernel(where, half_ref, other_ref, gain_ref, wg_ref, wu_ref, stream_ref, *outs):
    px, pz, core = where[0], where[1], where[2]
    half, other = half_ref[...].astype(f32), other_ref[...].astype(f32)
    rows = jnp.concatenate(
        [jnp.where(core == 0, half, other), jnp.where(core == 0, other, half)], axis=0
    )
    for kz in range(4):
        for kx in range(4):
            stream_ref[((px + kx) % 4) * 4 + (pz + kz) % 4] = rows[kz, kx].astype(bf16)
    turned = jnp.stack([rows[:, k] for k in range(4)], axis=0)
    wide = jnp.where(core == 0, rows, turned).reshape(256, 448)
    squares = jnp.sum(wide * wide, axis=1, keepdims=True)
    hi = squares.astype(bf16).astype(f32)
    lane = lax.broadcasted_iota(jnp.int32, (256, 128), 1)
    tail = jnp.where(lane == 0, hi, jnp.where(lane == 1, squares - hi, 0.0)).astype(bf16)
    scaled = (wide * gain_ref[...].astype(f32)).astype(bf16)
    gate = jnp.dot(scaled, wg_ref[...], preferred_element_type=f32).astype(bf16)
    gate = gate.reshape(4, 4, 16, FF)
    tail = tail.reshape(4, 4, 16, 128)
    for k in range(4):
        outs[k][:, :, :FF] = gate[:, k]
        outs[k][:, :, 2 * FF :] = tail[:, k]
    up = jnp.dot(scaled, wu_ref[...], preferred_element_type=f32).astype(bf16)
    up = up.reshape(4, 4, 16, FF)
    for k in range(4):
        outs[k][:, :, FF : 2 * FF] = up[:, k]


def sum4(refs, at):
    a, b, c, d = (ref[at].astype(f32) for ref in refs)
    return (a + b) + (c + d)


def fold_kernel(*refs):
    for kb in range(4):
        s = sum4(refs[:4], kb)
        refs[4 + kb][:, : 2 * FF] = s[:, : 2 * FF].astype(bf16)
        squares = jnp.sum(s[:, 2 * FF :], axis=1, keepdims=True)
        hi = squares.astype(bf16).astype(f32)
        lane = lax.broadcasted_iota(jnp.int32, (16, 128), 1)
        tail = jnp.where(lane == 0, hi, jnp.where(lane == 1, squares - hi, 0.0))
        refs[4 + kb][:, 2 * FF :] = tail.astype(bf16)


def finish_kernel(r0, r1, r2, r3, out):
    s = sum4((r0, r1, r2, r3), ...)
    squares = jnp.sum(s[:, 2 * FF :], axis=1, keepdims=True)
    inverse = lax.rsqrt(squares / D + EPSILON)
    gate = s[:, :FF] * inverse
    up = s[:, FF : 2 * FF] * inverse
    out[...] = (gate / (1.0 + jnp.exp(-gate)) * up).astype(bf16)


def local(
    queries,
    own_latent,
    prefix_cache,
    block_home,
    row_prompt,
    chosen,
    value_up,
    out_weight,
    residual,
    norm_gain,
    gate_weight,
    up_weight,
):
    replica = lax.axis_index("dp")
    lane = lax.axis_index("tp")
    px, pz = replica // 4, replica % 4
    core = lane % 2
    me = replica * 8 + lane
    i32 = jnp.int32
    where = jnp.stack([px, pz, core]).astype(i32)

    q = queries.reshape(16, 16, KV).transpose(1, 0, 2).reshape(256, KV)
    q = jnp.concatenate([q, q[:, LAT:]], axis=1)
    own = jnp.concatenate([own_latent, own_latent[:, LAT:]], axis=1)
    chips = [[c + 2 * y for y in range(4)] for c in range(2)]
    q_all = lax.all_gather(q, "tp", axis_index_groups=chips)

    slots = me * 16 + jnp.arange(16, dtype=i32)
    ids = jnp.arange(2048, dtype=i32)
    held = jnp.sum(jnp.where(block_home[None, :] == slots[:, None], ids[None, :], 0), axis=1)
    wanted = (row_prompt[:, None] * PB + chosen).reshape(16, 512)
    needed = jnp.any(wanted[:, None, :] == held[None, :, None], axis=2)
    offs = jnp.arange(16, dtype=i32)
    before = jnp.sum(
        jnp.where(needed[:, None, :] & (offs[None, :] < offs[:, None])[None], 1, 0), axis=2
    )
    places = jnp.arange(CAP, dtype=i32)
    picks = jnp.sum(
        jnp.where(needed[:, None, :] & (before[:, None, :] == places[None, :, None]), offs, 0),
        axis=2,
    )
    sent = call(
        fetch_kernel,
        "fetch",
        [shape(8, 288, 128)] * 4,
        [where, picks.reshape(-1), prefix_cache.reshape(16, BS, KV)],
        scalars=2,
    )
    got = [sent[0]] + [send_dp(sent[k], 0, k) for k in (1, 2, 3)]
    groups = call(regroup_kernel, "regroup", [shape(8, 288, 128)] * 4, got)
    arrived = {0: groups[0]}
    for k in (2, 1, 3):
        arrived[k] = send_dp(groups[k], 1, k)
    pieces = []
    for k in (0, 2, 1, 3):
        pieces += [arrived[k], swap_core(arrived[k])]

    prompt = lax.dynamic_slice_in_dim(row_prompt, replica * 16, 1, 0)[0]
    home = lax.dynamic_slice_in_dim(block_home, prompt * PB, PB, 0)
    my_chosen = lax.dynamic_slice_in_dim(chosen, replica * 16, 16, 0)
    sel = jnp.any(my_chosen[:, :, None] == jnp.arange(PB, dtype=i32)[None, None, :], axis=1)
    need = jnp.any(sel, axis=0)
    holder = home // 16
    rank = jnp.sum(
        jnp.where(
            need[None, :] & (holder[None, :] == holder[:, None]) & (home[None, :] < home[:, None]),
            1,
            0,
        ),
        axis=1,
    )
    kb = jnp.array([0, 2, 1, 3], i32)[:, None, None, None]
    from_core = core ^ jnp.array([0, 1], i32)[None, :, None, None]
    ka = jnp.arange(4, dtype=i32)[None, None, :, None]
    place = jnp.array([0, 1], i32)[None, None, None, :]
    kx = jnp.where(from_core == 0, ka, kb)
    kz = jnp.where(from_core == 0, kb, ka)
    dev = (((px - kx) % 4) * 4 + (pz - kz) % 4) * 8 + (lane - core + from_core)
    want_key = (dev * 2 + place).reshape(64)
    key = jnp.where(need, holder * 2 + rank, -1)
    hit = key[:, None] == want_key[None, :]
    use = jnp.dot(sel.astype(bf16), hit.astype(bf16), preferred_element_type=f32).astype(bf16)
    token = jnp.arange(4096, dtype=i32)
    slot_of = (token // 1024) * 16 + (token // 32) % 16
    spread = (jnp.arange(64, dtype=i32)[:, None] == slot_of[None, :]).astype(bf16)
    bias = (jnp.dot(use, spread, preferred_element_type=f32) - 1.0) * -NEG

    y = lane // 2
    parts = []
    for k in (2, 1, 3, 0):
        (o,) = attend((y ^ k).reshape(1), q_all, bias, pieces)
        parts.append(send_y(o, k) if k else o)
    per_head = merge(parts, q, own, value_up)

    near = [per_head] + [send_dp(per_head, 0, 4 - k) for k in (1, 2, 3)]
    near = jnp.concatenate(near, axis=0)
    far = [near] + [send_dp(near, 1, 4 - k) for k in (1, 2, 3)]
    keep, give = call(
        project_kernel,
        "project",
        [shape(2, 4, 16, 448, dtype=f32), shape(2, 4, 16, 448)],
        [where, *far, out_weight.T],
        scalars=1,
    )
    pair = (keep + swap_core(give).astype(f32)).astype(bf16)
    terms = [send_y(pair, k) for k in (1, 2, 3)]
    (half,) = call(
        join_kernel,
        "join",
        [shape(2, 4, 16, 448)],
        [where, pair, *terms, residual.reshape(16, 16, 448)],
        scalars=1,
    )
    other = swap_core(half)
    stream, *sums = call(
        ffn_kernel,
        "ffn",
        [shape(16, 16, 448)] + [shape(4, 16, 2 * FF + 128)] * 4,
        [where, half, other, norm_gain.reshape(1, 448), gate_weight, up_weight],
        scalars=1,
        limit=30,
    )
    got = [sums[0]] + [send_dp(sums[k], 0, k) for k in (2, 1, 3)]
    sums = call(fold_kernel, "fold", [shape(16, 2 * FF + 128)] * 4, got)
    got = [sums[0]] + [send_dp(sums[k], 1, k) for k in (2, 1, 3)]
    (hidden,) = call(finish_kernel, "finish", [shape(16, FF)], got)
    return (stream.reshape(256, 448), hidden)


def solution(mesh):
    placed = (
        P("dp", "tp"),
        P("dp", None),
        P(("dp", "tp"), None),
        P(),
        P(),
        P(),
        P("tp", None, None),
        P("tp", "dp"),
        P(None, "dp"),
        P("dp"),
        P("dp", "tp"),
        P("dp", "tp"),
    )
    return jax.shard_map(
        local, mesh=mesh, in_specs=placed, out_specs=(P(None, "dp"), P("dp", "tp")), check_vma=False
    )
```

```python
import functools
import math

import jax
import jax.numpy as jnp
from jax import lax
from jax.experimental import pallas as pl
from jax.experimental.pallas import tpu as pltpu
from jax.sharding import PartitionSpec as P

D = 7168
LAT = 512
ROPE = 64
QK_NOPE = 128
CAP = 2
PB = 512
BS = 64
KV = LAT + ROPE
EPSILON = 1e-06
FF = 2304
SCALE = 1.0 / math.sqrt(QK_NOPE + ROPE)
SCALE2 = SCALE / math.log(2.0)
NEG = -1e30
f32 = jnp.float32
bf16 = jnp.bfloat16


def send(x, axis, to, n):
    return lax.ppermute(x, axis, [(i, to(i)) for i in range(n)])


def swap_core(x):
    return send(x, "tp", lambda i: i ^ 1, 8)


def send_y(x, k):
    return send(x, "tp", lambda i: i ^ (2 * k), 8)


def send_dp(x, stage, k):
    pairs = []
    for i in range(128):
        dp, tp = i // 8, i % 8
        if tp % 2 == stage:
            to = ((dp // 4 + k) % 4) * 4 + dp % 4
        else:
            to = (dp // 4) * 4 + (dp % 4 + k) % 4
        pairs.append((i, to * 8 + tp))
    return lax.ppermute(x, ("dp", "tp"), pairs)


VMEM = pl.BlockSpec(memory_space=pltpu.VMEM)
SMEM = pl.BlockSpec(memory_space=pltpu.SMEM)
ANY = pl.BlockSpec(memory_space=pl.ANY)


def call(kernel, name, outs, ins, scalars=0, anys=0, limit=20, **kw):
    return pl.pallas_call(
        kernel,
        out_shape=outs,
        in_specs=[SMEM] * scalars + [VMEM] * (len(ins) - scalars - anys) + [ANY] * anys,
        out_specs=[VMEM] * len(outs),
        compiler_params=pltpu.CompilerParams(vmem_limit_bytes=limit * 1024 * 1024),
        name=name,
        **kw,
    )(*ins)


def shape(*dims, dtype=bf16):
    return jax.ShapeDtypeStruct(dims, dtype)


def place_of(where, ka, kb):
    px, pz, core = where[0], where[1], where[2]
    kx = jnp.where(core == 0, ka, kb)
    kz = jnp.where(core == 0, kb, ka)
    return ((px + kx) % 4) * 4 + (pz + kz) % 4


def fetch_kernel(where, picks, tokens, *outs):
    for ka in range(4):
        for kb in range(4):
            dest = place_of(where, ka, kb)
            for rank in range(CAP):
                pick = picks[dest * CAP + rank]
                out = outs[ka]
                at = kb * CAP + rank
                for c in range(4):
                    out[at, c * BS : (c + 1) * BS, :] = tokens[pick, :, c * 128 : (c + 1) * 128]
                rope = tokens[pick, :, LAT:KV]
                out[at, 4 * BS :, :] = jnp.concatenate([rope[:32], rope[32:]], axis=1)


def regroup_kernel(*refs):
    for ka in range(4):
        for kb in range(4):
            refs[4 + kb][ka * CAP : (ka + 1) * CAP] = refs[ka][kb * CAP : (kb + 1) * CAP]


def half_latent(refs, half):
    rows = []
    for ref in refs:
        parts = [
            ref[:, c * BS + half * 32 : c * BS + half * 32 + 32, :].reshape(-1, 128)
            for c in range(4)
        ]
        rows.append(jnp.concatenate(parts, axis=1))
    return jnp.concatenate(rows, axis=0)


def half_rope(refs, half):
    rope = jnp.concatenate(
        [ref[:, 4 * BS : 4 * BS + 32, :].reshape(-1, 128) for ref in refs], axis=0
    )
    lane = lax.broadcasted_iota(jnp.int32, rope.shape, 1)
    keep = (lane < ROPE) if half == 0 else (lane >= ROPE)
    return jnp.where(keep, rope, jnp.zeros_like(rope))


def attend_kernel(groups, resume, last, *refs):
    index, q_ref, use_ref = refs[:3]
    pieces = refs[3 : 3 + 2 * groups]
    refs = refs[3 + 2 * groups :]
    if resume:
        acc_in, stat_in = refs[0], refs[1]
        refs = refs[2:]
    m_rows = q_ref.shape[1]
    chips = [index[0]] if last else list(range(4))
    slot = lax.broadcasted_iota(jnp.int32, (16, 1024), 0)
    token = lax.broadcasted_iota(jnp.int32, (16, 1024), 1)
    spread = ((token // 32) % 16 == slot).astype(f32).astype(bf16)
    biases = [
        (jnp.dot(use_ref[g], spread, preferred_element_type=f32) - 1.0) * -NEG
        for g in range(groups)
    ]

    def values(g):
        mine = pieces[2 * g : 2 * g + 2]
        return jnp.concatenate([half_latent(mine, 0), half_latent(mine, 1)], axis=0)

    def scores(chip, g):
        mine = pieces[2 * g : 2 * g + 2]
        ropes = jnp.concatenate([half_rope(mine, 0), half_rope(mine, 1)], axis=0)
        keys = jnp.concatenate([values(g), ropes], axis=1)
        s = lax.dot_general(
            q_ref[chip], keys, (((1,), (1,)), ((), ())), preferred_element_type=f32
        )
        n = s.shape[1]
        return (s.reshape(m_rows // 16, 16, n) + biases[g][None]).reshape(m_rows, n)

    steps = [(chip, g) for chip in chips for g in range(groups)]
    s = scores(*steps[0])
    for i, (chip, g) in enumerate(steps):
        ahead = scores(*steps[i + 1]) if i + 1 < len(steps) else None
        if g == 0:
            top = total = acc = None
            if resume:
                top, total = stat_in[chip, :, 0:1], stat_in[chip, :, 64:65]
                acc = acc_in[chip]
        high = jnp.max(s, axis=1, keepdims=True)
        new = high if top is None else jnp.maximum(top, high)
        p = jnp.exp2((s - new) * SCALE2)
        part = jnp.sum(p, axis=1, keepdims=True)
        o = jnp.dot(p.astype(bf16), values(g), preferred_element_type=f32)
        if top is None:
            acc, total = o, part
        else:
            fade = jnp.exp2((top - new) * SCALE2)
            acc, total = acc * fade + o, total * fade + part
        top, s = new, ahead
        if g == groups - 1 and not last:
            lane = lax.broadcasted_iota(jnp.int32, (m_rows, 128), 1)
            refs[0][chip] = acc
            refs[1][chip] = jnp.where(lane < 64, top, total)
    if not last:
        return
    out_ref = refs[0]
    out_ref[:m_rows] = (acc / total).astype(bf16)
    lse = top * SCALE + jnp.log(total)
    hi = lse.astype(bf16).astype(f32)
    mid = (lse - hi).astype(bf16).astype(f32)
    low = lse - hi - mid
    lane = lax.broadcasted_iota(jnp.int32, (m_rows, 128), 1)
    stats = jnp.where(lane == 0, hi, jnp.where(lane == 1, mid, jnp.where(lane == 2, low, 0.0)))
    stats = stats.T[:16]
    out_ref[m_rows:] = jnp.concatenate([stats, jnp.zeros_like(stats)], axis=1).astype(bf16)


def attend(index, q, use, pieces, carry=(), last=True):
    m_rows = q.shape[1]
    groups = len(pieces) // 2
    if last:
        outs = [shape(m_rows + 16, LAT)]
    else:
        outs = [shape(4, m_rows, LAT, dtype=f32), shape(4, m_rows, 128, dtype=f32)]
    chips = 1 if last else 4
    cost = pl.CostEstimate(
        flops=2 * chips * m_rows * groups * 1024 * (768 + 512) * 2,
        bytes_accessed=groups * 16 * 288 * 128 * 2,
        transcendentals=chips * m_rows * groups * 1024,
    )
    return call(
        functools.partial(attend_kernel, groups, bool(carry), last),
        "attend",
        outs,
        [index, q, use, *pieces, *carry],
        scalars=1,
        limit=28,
        cost_estimate=cost,
    )


def merge_kernel(o0, o1, o2, o3, q_ref, own_ref, up_ref, out_ref):
    heads, rows = 16, 16
    own = own_ref[...].astype(f32)
    q = q_ref[...].astype(f32).reshape(heads, rows, 640)
    lane = lax.broadcasted_iota(jnp.int32, (rows, 640), 1)
    key = jnp.where(lane < KV, own, 0.0)
    s_own = jnp.sum(q * key[None], axis=2, keepdims=True).reshape(heads * rows, 1) * SCALE
    lses = []
    for o in (o0, o1, o2, o3):
        row = jnp.sum(o[256:, :256].astype(f32), axis=0, keepdims=True)
        lses.append(jnp.broadcast_to(row, (128, 256)).T[:, :1])
    top = s_own
    for v in lses:
        top = jnp.maximum(top, v)
    e_own = jnp.exp(s_own - top)
    es = [jnp.exp(v - top) for v in lses]
    den = e_own + ((es[0] + es[1]) + (es[2] + es[3]))
    mix = (e_own / den).reshape(heads, rows, 1) * own[None, :, :LAT]
    mix = mix.reshape(heads * rows, LAT)
    for o, e in zip((o0, o1, o2, o3), es):
        mix = mix + (e / den) * o[:256].astype(f32)
    mix = mix.astype(bf16)
    for h in range(heads):
        out_ref[:, h * 128 : (h + 1) * 128] = jnp.dot(
            mix[h * rows : (h + 1) * rows], up_ref[h], preferred_element_type=f32
        ).astype(bf16)


def merge(parts, q, own, value_up):
    return pl.pallas_call(
        merge_kernel,
        out_shape=jax.ShapeDtypeStruct((16, 2048), bf16),
        in_specs=[pl.BlockSpec(memory_space=pltpu.VMEM)] * 7,
        out_specs=pl.BlockSpec(memory_space=pltpu.VMEM),
        compiler_params=pltpu.CompilerParams(vmem_limit_bytes=24 * 1024 * 1024),
        name="merge",
    )(*parts, q, own, value_up)


def project_kernel(where, p0, p1, p2, p3, weight, keep_ref, give_ref):
    core = where[2]
    rows = jnp.concatenate([p0[...], p1[...], p2[...], p3[...]], axis=0)
    full = lax.dot_general(
        rows, weight[...], (((1,), (1,)), ((), ())), preferred_element_type=f32
    ).reshape(4, 4, 16, 448)

    @pl.when(core == 0)
    def _():
        keep_ref[...] = full[:2]
        give_ref[...] = full[2:].astype(bf16)

    @pl.when(core == 1)
    def _():
        for i in range(2):
            keep_ref[i] = full[:, 2 + i]
            give_ref[i] = full[:, i].astype(bf16)


def join_kernel(where, pair, t1, t2, t3, residual, out):
    px, pz, core = where[0], where[1], where[2]
    for i in range(2):
        for kx in range(4):
            kz = core * 2 + i
            dp = ((px + kx) % 4) * 4 + (pz + kz) % 4
            attn = (pair[i, kx].astype(f32) + t1[i, kx].astype(f32)) + (
                t2[i, kx].astype(f32) + t3[i, kx].astype(f32)
            )
            out[i, kx] = (residual[dp].astype(f32) + attn).astype(bf16)


def ffn_kernel(where, half_ref, other_ref, gain_ref, wg_ref, wu_any, stream_ref, *outs):
    *outs, wu_ref, sem = outs
    bring = pltpu.make_async_copy(wu_any, wu_ref, sem)
    bring.start()
    px, pz, core = where[0], where[1], where[2]
    half, other = half_ref[...].astype(f32), other_ref[...].astype(f32)
    rows = jnp.concatenate(
        [jnp.where(core == 0, half, other), jnp.where(core == 0, other, half)], axis=0
    )
    for kz in range(4):
        for kx in range(4):
            stream_ref[((px + kx) % 4) * 4 + (pz + kz) % 4] = rows[kz, kx].astype(bf16)
    turned = jnp.stack([rows[:, k] for k in range(4)], axis=0)
    wide = jnp.where(core == 0, rows, turned).reshape(256, 448)
    squares = jnp.sum(wide * wide, axis=1, keepdims=True)
    hi = squares.astype(bf16).astype(f32)
    lane = lax.broadcasted_iota(jnp.int32, (256, 128), 1)
    tail = jnp.where(lane == 0, hi, jnp.where(lane == 1, squares - hi, 0.0)).astype(bf16)
    scaled = (wide * gain_ref[...].astype(f32)).astype(bf16)
    gate = jnp.dot(scaled, wg_ref[...], preferred_element_type=f32).astype(bf16)
    gate = gate.reshape(4, 4, 16, FF)
    tail = tail.reshape(4, 4, 16, 128)
    for k in range(4):
        outs[k][:, :, :FF] = gate[:, k]
        outs[k][:, :, 2 * FF :] = tail[:, k]
    bring.wait()
    up = jnp.dot(scaled, wu_ref[...], preferred_element_type=f32).astype(bf16)
    up = up.reshape(4, 4, 16, FF)
    for k in range(4):
        outs[k][:, :, FF : 2 * FF] = up[:, k]


def sum4(refs, at):
    a, b, c, d = (ref[at].astype(f32) for ref in refs)
    return (a + b) + (c + d)


def fold_kernel(*refs):
    for kb in range(4):
        s = sum4(refs[:4], kb)
        refs[4 + kb][:, : 2 * FF] = s[:, : 2 * FF].astype(bf16)
        squares = jnp.sum(s[:, 2 * FF :], axis=1, keepdims=True)
        hi = squares.astype(bf16).astype(f32)
        lane = lax.broadcasted_iota(jnp.int32, (16, 128), 1)
        tail = jnp.where(lane == 0, hi, jnp.where(lane == 1, squares - hi, 0.0))
        refs[4 + kb][:, 2 * FF :] = tail.astype(bf16)


def finish_kernel(r0, r1, r2, r3, out):
    s = sum4((r0, r1, r2, r3), ...)
    squares = jnp.sum(s[:, 2 * FF :], axis=1, keepdims=True)
    inverse = lax.rsqrt(squares / D + EPSILON)
    gate = s[:, :FF] * inverse
    up = s[:, FF : 2 * FF] * inverse
    out[...] = (gate / (1.0 + jnp.exp(-gate)) * up).astype(bf16)


def local(
    queries,
    own_latent,
    prefix_cache,
    block_home,
    row_prompt,
    chosen,
    value_up,
    out_weight,
    residual,
    norm_gain,
    gate_weight,
    up_weight,
):
    replica = lax.axis_index("dp")
    lane = lax.axis_index("tp")
    px, pz = replica // 4, replica % 4
    core = lane % 2
    me = replica * 8 + lane
    i32 = jnp.int32
    where = jnp.stack([px, pz, core]).astype(i32)

    q = queries.reshape(16, 16, KV).transpose(1, 0, 2).reshape(256, KV)
    q = jnp.concatenate([q, q[:, LAT:]], axis=1)
    own = jnp.concatenate([own_latent, own_latent[:, LAT:]], axis=1)
    chips = [[c + 2 * y for y in range(4)] for c in range(2)]
    q_all = lax.all_gather(q, "tp", axis_index_groups=chips)

    slots = me * 16 + jnp.arange(16, dtype=i32)
    ids = jnp.arange(2048, dtype=i32)
    held = jnp.sum(jnp.where(block_home[None, :] == slots[:, None], ids[None, :], 0), axis=1)
    wanted = (row_prompt[:, None] * PB + chosen).reshape(16, 512)
    needed = jnp.any(wanted[:, None, :] == held[None, :, None], axis=2)
    offs = jnp.arange(16, dtype=i32)
    before = jnp.sum(
        jnp.where(needed[:, None, :] & (offs[None, :] < offs[:, None])[None], 1, 0), axis=2
    )
    places = jnp.arange(CAP, dtype=i32)
    picks = jnp.sum(
        jnp.where(needed[:, None, :] & (before[:, None, :] == places[None, :, None]), offs, 0),
        axis=2,
    )
    sent = call(
        fetch_kernel,
        "fetch",
        [shape(8, 288, 128)] * 4,
        [where, picks.reshape(-1), prefix_cache.reshape(16, BS, KV)],
        scalars=2,
    )
    got = [sent[0]] + [send_dp(sent[k], 0, k) for k in (1, 2, 3)]

    prompt = lax.dynamic_slice_in_dim(row_prompt, replica * 16, 1, 0)[0]
    home = lax.dynamic_slice_in_dim(block_home, prompt * PB, PB, 0)
    my_chosen = lax.dynamic_slice_in_dim(chosen, replica * 16, 16, 0)
    sel = jnp.any(my_chosen[:, :, None] == jnp.arange(PB, dtype=i32)[None, None, :], axis=1)
    need = jnp.any(sel, axis=0)
    holder = home // 16
    rank = jnp.sum(
        jnp.where(
            need[None, :] & (holder[None, :] == holder[:, None]) & (home[None, :] < home[:, None]),
            1,
            0,
        ),
        axis=1,
    )
    kb = jnp.array([0, 2, 1, 3], i32)[:, None, None, None]
    from_core = core ^ jnp.array([0, 1], i32)[None, :, None, None]
    ka = jnp.arange(4, dtype=i32)[None, None, :, None]
    place = jnp.array([0, 1], i32)[None, None, None, :]
    kx = jnp.where(from_core == 0, ka, kb)
    kz = jnp.where(from_core == 0, kb, ka)
    dev = (((px - kx) % 4) * 4 + (pz - kz) % 4) * 8 + (lane - core + from_core)
    want_key = (dev * 2 + place).reshape(64)
    key = jnp.where(need, holder * 2 + rank, -1)
    hit = key[:, None] == want_key[None, :]
    use = jnp.dot(sel.astype(bf16), hit.astype(bf16), preferred_element_type=f32).astype(bf16)
    use = use.reshape(16, 4, 16).transpose(1, 0, 2)

    got[0], use = lax.optimization_barrier((got[0], use))
    groups = call(regroup_kernel, "regroup", [shape(8, 288, 128)] * 4, got)
    arrived = {0: groups[0]}
    for k in (2, 1, 3):
        arrived[k] = send_dp(groups[k], 1, k)
    pieces = {k: [arrived[k], swap_core(arrived[k])] for k in (0, 2, 1, 3)}
    y = lane // 2
    carry = attend(y.reshape(1), q_all, use[0:1], pieces[0], last=False)
    carry = attend(y.reshape(1), q_all, use[1:2], pieces[2], carry, last=False)
    parts = []
    for k in (2, 1, 3, 0):
        index = (y ^ k).reshape(1)
        (o,) = attend(index, q_all, use[2:4], pieces[1] + pieces[3], carry)
        parts.append(send_y(o, k) if k else o)
    per_head = merge(parts, q, own, value_up)

    near = [per_head] + [send_dp(per_head, 0, 4 - k) for k in (1, 2, 3)]
    near = jnp.concatenate(near, axis=0)
    far = [near] + [send_dp(near, 1, 4 - k) for k in (1, 2, 3)]
    keep, give = call(
        project_kernel,
        "project",
        [shape(2, 4, 16, 448, dtype=f32), shape(2, 4, 16, 448)],
        [where, *far, out_weight.T],
        scalars=1,
    )
    pair = (keep + swap_core(give).astype(f32)).astype(bf16)
    terms = [send_y(pair, k) for k in (1, 2, 3)]
    (half,) = call(
        join_kernel,
        "join",
        [shape(2, 4, 16, 448)],
        [where, pair, *terms, residual.reshape(16, 16, 448)],
        scalars=1,
    )
    other = swap_core(half)
    stream, *sums = call(
        ffn_kernel,
        "ffn",
        [shape(16, 16, 448)] + [shape(4, 16, 2 * FF + 128)] * 4,
        [where, half, other, norm_gain.reshape(1, 448), gate_weight, up_weight],
        scalars=1,
        anys=1,
        limit=30,
        scratch_shapes=[pltpu.VMEM((448, FF), bf16), pltpu.SemaphoreType.DMA(())],
    )
    got = [sums[0]] + [send_dp(sums[k], 0, k) for k in (2, 1, 3)]
    sums = call(fold_kernel, "fold", [shape(16, 2 * FF + 128)] * 4, got)
    got = [sums[0]] + [send_dp(sums[k], 1, k) for k in (2, 1, 3)]
    (hidden,) = call(finish_kernel, "finish", [shape(16, FF)], got)
    return (stream.reshape(256, 448), hidden)


def solution(mesh):
    placed = (
        P("dp", "tp"),
        P("dp", None),
        P(("dp", "tp"), None),
        P(),
        P(),
        P(),
        P("tp", None, None),
        P("tp", "dp"),
        P(None, "dp"),
        P("dp"),
        P("dp", "tp"),
        P("dp", "tp"),
    )
    return jax.shard_map(
        local, mesh=mesh, in_specs=placed, out_specs=(P(None, "dp"), P("dp", "tp")), check_vma=False
    )
```

```python
import functools
import math

import jax
import jax.numpy as jnp
from jax import lax
from jax.experimental import pallas as pl
from jax.experimental.pallas import tpu as pltpu
from jax.sharding import PartitionSpec as P

D = 7168
LAT = 512
ROPE = 64
QK_NOPE = 128
CAP = 2
PB = 512
BS = 64
KV = LAT + ROPE
EPSILON = 1e-06
FF = 2304
SCALE = 1.0 / math.sqrt(QK_NOPE + ROPE)
SCALE2 = SCALE / math.log(2.0)
NEG = -1e30
f32 = jnp.float32
bf16 = jnp.bfloat16


def send(x, axis, to, n):
    return lax.ppermute(x, axis, [(i, to(i)) for i in range(n)])


def swap_core(x):
    return send(x, "tp", lambda i: i ^ 1, 8)


def send_y(x, k):
    return send(x, "tp", lambda i: i ^ (2 * k), 8)


def send_dp(x, stage, k):
    pairs = []
    for i in range(128):
        dp, tp = i // 8, i % 8
        if tp % 2 == stage:
            to = ((dp // 4 + k) % 4) * 4 + dp % 4
        else:
            to = (dp // 4) * 4 + (dp % 4 + k) % 4
        pairs.append((i, to * 8 + tp))
    return lax.ppermute(x, ("dp", "tp"), pairs)


VMEM = pl.BlockSpec(memory_space=pltpu.VMEM)
SMEM = pl.BlockSpec(memory_space=pltpu.SMEM)
ANY = pl.BlockSpec(memory_space=pl.ANY)


def call(kernel, name, outs, ins, scalars=0, anys=0, limit=20, **kw):
    return pl.pallas_call(
        kernel,
        out_shape=outs,
        in_specs=[SMEM] * scalars + [VMEM] * (len(ins) - scalars - anys) + [ANY] * anys,
        out_specs=[VMEM] * len(outs),
        compiler_params=pltpu.CompilerParams(vmem_limit_bytes=limit * 1024 * 1024),
        name=name,
        **kw,
    )(*ins)


def shape(*dims, dtype=bf16):
    return jax.ShapeDtypeStruct(dims, dtype)


def place_of(where, ka, kb):
    px, pz, core = where[0], where[1], where[2]
    kx = jnp.where(core == 0, ka, kb)
    kz = jnp.where(core == 0, kb, ka)
    return ((px + kx) % 4) * 4 + (pz + kz) % 4


def plan_kernel(where, prompts, home_ref, prompt_ref, chosen_ref, picks_ref, use_ref):
    px, pz, core, lane = where[0], where[1], where[2], where[3]
    replica = px * 4 + pz
    i32 = jnp.int32
    home = home_ref[...].reshape(16, 128)
    ids = lax.broadcasted_iota(i32, (16, 128), 0) * 128 + lax.broadcasted_iota(i32, (16, 128), 1)
    chosen = chosen_ref[...]
    wanted = chosen + prompt_ref[...] * PB
    asked = []
    for slot in range(16):
        found = home == (replica * 8 + lane) * 16 + slot
        block = jnp.sum(jnp.where(found, ids, 0), axis=(0, 1), keepdims=True)
        asked.append(jnp.max(jnp.where(wanted == block, 1.0, 0.0), axis=0, keepdims=True))
    asked = jnp.concatenate(asked, axis=0).astype(bf16)
    row = lax.broadcasted_iota(i32, (256, 128), 0)
    owner = lax.broadcasted_iota(i32, (256, 128), 1)
    owns = jnp.where(row // 16 == owner, 1.0, 0.0).astype(bf16)
    needed = jnp.dot(asked, owns, preferred_element_type=f32) > 0.5
    flag = jnp.where(needed, 1.0, 0.0)
    slot = lax.broadcasted_iota(i32, (16, 128), 0)
    low = lax.broadcasted_iota(i32, (16, 16), 0) > lax.broadcasted_iota(i32, (16, 16), 1)
    low = jnp.where(low, 1.0, 0.0).astype(bf16)
    before = jnp.dot(low, flag.astype(bf16), preferred_element_type=f32)
    for rank in range(CAP):
        pick = needed & (before > rank - 0.5) & (before < rank + 0.5)
        picks_ref[rank : rank + 1] = jnp.sum(jnp.where(pick, slot, 0), axis=0, keepdims=True)

    mine = pltpu.roll(chosen, (256 - replica * 16) % 256, 1)[:, :128]
    mine = jnp.concatenate([mine.astype(f32), jnp.zeros((96, 128), f32)], axis=0).T[:16]
    block = lax.broadcasted_iota(i32, (16, PB), 1).astype(f32)
    uses = jnp.zeros((16, PB), f32)
    for t in range(32):
        uses = jnp.where(mine[:, t : t + 1] == block, 1.0, uses)
    need = jnp.max(uses, axis=0, keepdims=True) > 0.5
    here = home_ref[prompts[replica * 16]]
    here = jnp.concatenate([here[i : i + 1] for i in range(4)], axis=1)
    holder = here // 16
    live = jnp.where(need, here, -1).astype(f32)
    column = jnp.broadcast_to(live, (128, PB)).T[:, :1].astype(i32)
    fewer = (column // 16 == holder) & (column < here) & (column >= 0)
    rank = jnp.sum(jnp.where(fewer, 1, 0), axis=0, keepdims=True)
    key = jnp.where(need, holder * CAP + rank, -1)
    at = lax.broadcasted_iota(i32, (64, PB), 0)
    kb = at // 16
    kb = jnp.where(kb == 2, 3, jnp.where(kb == 3, 2, kb))
    sib, ka, place = (at // 8) % 2, (at // 2) % 4, at % 2
    from_core = core ^ sib
    kx = jnp.where(from_core == 0, ka, kb)
    kz = jnp.where(from_core == 0, kb, ka)
    dev = (((px + 4 - kx) % 4) * 4 + (pz + 4 - kz) % 4) * 8 + lane - core + from_core
    hit = jnp.where(dev * CAP + place == key, 1.0, 0.0).astype(bf16)
    use = lax.dot_general(
        uses.astype(bf16), hit, (((1,), (1,)), ((), ())), preferred_element_type=f32
    )
    use_ref[...] = use.astype(bf16)


def fetch_kernel(where, picks, tokens, *outs):
    for ka in range(4):
        for kb in range(4):
            dest = place_of(where, ka, kb)
            for rank in range(CAP):
                pick = picks[rank, dest]
                out = outs[ka]
                at = kb * CAP + rank
                for c in range(4):
                    out[at, c * BS : (c + 1) * BS, :] = tokens[pick, :, c * 128 : (c + 1) * 128]
                rope = tokens[pick, :, LAT:KV]
                out[at, 4 * BS :, :] = jnp.concatenate([rope[:32], rope[32:]], axis=1)


def regroup_kernel(*refs):
    refs = refs[:4] + refs[8:]
    for ka in range(4):
        for kb in range(4):
            refs[4 + kb][ka * CAP : (ka + 1) * CAP] = refs[ka][kb * CAP : (kb + 1) * CAP]


def after_kernel(_, *refs):
    count = len(refs) // 2
    for i in range(count):
        refs[count + i][...] = refs[i][...]


def after(first, *blocks):
    return call(after_kernel, "after", [shape(8, 288, 128)] * len(blocks), [first, *blocks])


def half_latent(refs, half):
    rows = []
    for ref in refs:
        parts = [
            ref[:, c * BS + half * 32 : c * BS + half * 32 + 32, :].reshape(-1, 128)
            for c in range(4)
        ]
        rows.append(jnp.concatenate(parts, axis=1))
    return jnp.concatenate(rows, axis=0)


def half_rope(refs, half):
    rope = jnp.concatenate(
        [ref[:, 4 * BS : 4 * BS + 32, :].reshape(-1, 128) for ref in refs], axis=0
    )
    lane = lax.broadcasted_iota(jnp.int32, rope.shape, 1)
    keep = (lane < ROPE) if half == 0 else (lane >= ROPE)
    return jnp.where(keep, rope, jnp.zeros_like(rope))


def attend_kernel(first, groups, chips, resume, last, *refs):
    use_ref, refs = refs[0], refs[1:]
    qs, refs = dict(zip(chips, refs)), refs[len(chips) :]
    pieces, refs = refs[: 2 * groups], refs[2 * groups :]
    if resume:
        (acc_in, stat_in), refs = refs[:2], refs[2:]
    m_rows = 256
    slot = lax.broadcasted_iota(jnp.int32, (64, 1024), 0)
    token = lax.broadcasted_iota(jnp.int32, (64, 1024), 1)
    biases = []
    for g in range(groups):
        spread = ((token // 32) % 16 + 16 * (first + g) == slot).astype(f32).astype(bf16)
        used = jnp.dot(use_ref[...], spread, preferred_element_type=f32)
        biases.append((used - 1.0) * -NEG)

    def values(g):
        mine = pieces[2 * g : 2 * g + 2]
        return jnp.concatenate([half_latent(mine, 0), half_latent(mine, 1)], axis=0)

    def scores(chip, g):
        mine = pieces[2 * g : 2 * g + 2]
        ropes = jnp.concatenate([half_rope(mine, 0), half_rope(mine, 1)], axis=0)
        keys = jnp.concatenate([values(g), ropes], axis=1)
        s = lax.dot_general(
            qs[chip][...], keys, (((1,), (1,)), ((), ())), preferred_element_type=f32
        )
        n = s.shape[1]
        return (s.reshape(m_rows // 16, 16, n) + biases[g][None]).reshape(m_rows, n)

    steps = [(chip, g) for chip in chips for g in range(groups)]
    s = scores(*steps[0])
    for i, (chip, g) in enumerate(steps):
        ahead = scores(*steps[i + 1]) if i + 1 < len(steps) else None
        if g == 0:
            top = total = acc = None
            if resume:
                top, total = stat_in[chip, :, 0:1], stat_in[chip, :, 64:65]
                acc = acc_in[chip]
        high = jnp.max(s, axis=1, keepdims=True)
        new = high if top is None else jnp.maximum(top, high)
        p = jnp.exp2((s - new) * SCALE2)
        part = jnp.sum(p, axis=1, keepdims=True)
        o = jnp.dot(p.astype(bf16), values(g), preferred_element_type=f32)
        if top is None:
            acc, total = o, part
        else:
            fade = jnp.exp2((top - new) * SCALE2)
            acc, total = acc * fade + o, total * fade + part
        top, s = new, ahead
        if g == groups - 1 and not last:
            lane = lax.broadcasted_iota(jnp.int32, (m_rows, 128), 1)
            refs[0][chip] = acc
            refs[1][chip] = jnp.where(lane < 64, top, total)
    if not last:
        refs[2][...] = jnp.zeros((8, 128), f32)
        return
    out_ref = refs[0]
    out_ref[:m_rows] = (acc / total).astype(bf16)
    lse = top * SCALE + jnp.log(total)
    hi = lse.astype(bf16).astype(f32)
    mid = (lse - hi).astype(bf16).astype(f32)
    low = lse - hi - mid
    lane = lax.broadcasted_iota(jnp.int32, (m_rows, 128), 1)
    stats = jnp.where(lane == 0, hi, jnp.where(lane == 1, mid, jnp.where(lane == 2, low, 0.0)))
    stats = stats.T[:16]
    out_ref[m_rows:] = jnp.concatenate([stats, jnp.zeros_like(stats)], axis=1).astype(bf16)


def attend(use, qs, first, pieces, carry=(), last=True):
    groups = len(pieces) // 2
    if last:
        outs = [shape(256 + 16, LAT)]
    else:
        outs = [shape(4, 256, LAT, dtype=f32), shape(4, 256, 128, dtype=f32)]
        outs.append(shape(8, 128, dtype=f32))
    return call(
        functools.partial(attend_kernel, first, groups, list(qs), bool(carry), last),
        "attend",
        outs,
        [use, *qs.values(), *pieces, *carry],
        limit=16,
    )


def merge_kernel(o0, o1, o2, o3, q_ref, own_ref, up_ref, out_ref):
    heads, rows = 16, 16
    own = own_ref[...].astype(f32)
    q = q_ref[...].astype(f32).reshape(heads, rows, 640)
    lane = lax.broadcasted_iota(jnp.int32, (rows, 640), 1)
    key = jnp.where(lane < KV, own, 0.0)
    s_own = jnp.sum(q * key[None], axis=2, keepdims=True).reshape(heads * rows, 1) * SCALE
    lses = []
    for o in (o0, o1, o2, o3):
        row = jnp.sum(o[256:, :256].astype(f32), axis=0, keepdims=True)
        lses.append(jnp.broadcast_to(row, (128, 256)).T[:, :1])
    top = s_own
    for v in lses:
        top = jnp.maximum(top, v)
    e_own = jnp.exp(s_own - top)
    es = [jnp.exp(v - top) for v in lses]
    den = e_own + ((es[0] + es[1]) + (es[2] + es[3]))
    mix = (e_own / den).reshape(heads, rows, 1) * own[None, :, :LAT]
    mix = mix.reshape(heads * rows, LAT)
    for o, e in zip((o0, o1, o2, o3), es):
        mix = mix + (e / den) * o[:256].astype(f32)
    mix = mix.astype(bf16)
    for h in range(heads):
        out_ref[:, h * 128 : (h + 1) * 128] = jnp.dot(
            mix[h * rows : (h + 1) * rows], up_ref[h], preferred_element_type=f32
        ).astype(bf16)


def merge(parts, q, own, value_up):
    return pl.pallas_call(
        merge_kernel,
        out_shape=jax.ShapeDtypeStruct((16, 2048), bf16),
        in_specs=[pl.BlockSpec(memory_space=pltpu.VMEM)] * 7,
        out_specs=pl.BlockSpec(memory_space=pltpu.VMEM),
        compiler_params=pltpu.CompilerParams(vmem_limit_bytes=24 * 1024 * 1024),
        name="merge",
    )(*parts, q, own, value_up)


def project_kernel(where, p0, p1, p2, p3, weight, keep_ref, give_ref):
    core = where[2]
    rows = jnp.concatenate([p0[...], p1[...], p2[...], p3[...]], axis=0)
    full = lax.dot_general(
        rows, weight[...], (((1,), (1,)), ((), ())), preferred_element_type=f32
    ).reshape(4, 4, 16, 448)

    @pl.when(core == 0)
    def _():
        keep_ref[...] = full[:2]
        give_ref[...] = full[2:].astype(bf16)

    @pl.when(core == 1)
    def _():
        for i in range(2):
            keep_ref[i] = full[:, 2 + i]
            give_ref[i] = full[:, i].astype(bf16)


def join_kernel(where, pair, t1, t2, t3, residual, out):
    px, pz, core = where[0], where[1], where[2]
    for i in range(2):
        for kx in range(4):
            kz = core * 2 + i
            dp = ((px + kx) % 4) * 4 + (pz + kz) % 4
            attn = (pair[i, kx].astype(f32) + t1[i, kx].astype(f32)) + (
                t2[i, kx].astype(f32) + t3[i, kx].astype(f32)
            )
            out[i, kx] = (residual[dp].astype(f32) + attn).astype(bf16)


def ffn_kernel(where, half_ref, other_ref, gain_ref, wg_any, wu_any, stream_ref, *outs):
    *outs, wg_ref, wu_ref, sem_g, sem_u = outs
    bring_g = pltpu.make_async_copy(wg_any, wg_ref, sem_g)
    bring_u = pltpu.make_async_copy(wu_any, wu_ref, sem_u)
    bring_g.start()
    bring_u.start()
    px, pz, core = where[0], where[1], where[2]
    half, other = half_ref[...].astype(f32), other_ref[...].astype(f32)
    rows = jnp.concatenate(
        [jnp.where(core == 0, half, other), jnp.where(core == 0, other, half)], axis=0
    )
    for kz in range(4):
        for kx in range(4):
            stream_ref[((px + kx) % 4) * 4 + (pz + kz) % 4] = rows[kz, kx].astype(bf16)
    turned = jnp.stack([rows[:, k] for k in range(4)], axis=0)
    wide = jnp.where(core == 0, rows, turned).reshape(256, 448)
    squares = jnp.sum(wide * wide, axis=1, keepdims=True)
    hi = squares.astype(bf16).astype(f32)
    lane = lax.broadcasted_iota(jnp.int32, (256, 128), 1)
    tail = jnp.where(lane == 0, hi, jnp.where(lane == 1, squares - hi, 0.0)).astype(bf16)
    scaled = (wide * gain_ref[...].astype(f32)).astype(bf16)
    bring_g.wait()
    gate = jnp.dot(scaled, wg_ref[...], preferred_element_type=f32).astype(bf16)
    gate = gate.reshape(4, 4, 16, FF)
    tail = tail.reshape(4, 4, 16, 128)
    for k in range(4):
        outs[k][:, :, :FF] = gate[:, k]
        outs[k][:, :, 2 * FF :] = tail[:, k]
    bring_u.wait()
    up = jnp.dot(scaled, wu_ref[...], preferred_element_type=f32).astype(bf16)
    up = up.reshape(4, 4, 16, FF)
    for k in range(4):
        outs[k][:, :, FF : 2 * FF] = up[:, k]


def turn_kernel(x, out):
    out[...] = x[...].astype(f32).T.astype(bf16)


def turn(x):
    return call(turn_kernel, "turn", [shape(x.shape[1], x.shape[0])], [x])[0]


def sum4(refs, at):
    a, b, c, d = (ref[at].astype(f32) for ref in refs)
    return (a + b) + (c + d)


def fold_kernel(*refs):
    for kb in range(4):
        s = sum4(refs[:4], kb)
        refs[4 + kb][:, : 2 * FF] = s[:, : 2 * FF].astype(bf16)
        squares = jnp.sum(s[:, 2 * FF :], axis=1, keepdims=True)
        hi = squares.astype(bf16).astype(f32)
        lane = lax.broadcasted_iota(jnp.int32, (16, 128), 1)
        tail = jnp.where(lane == 0, hi, jnp.where(lane == 1, squares - hi, 0.0))
        refs[4 + kb][:, 2 * FF :] = tail.astype(bf16)


def finish_kernel(r0, r1, r2, r3, out):
    s = sum4((r0, r1, r2, r3), ...)
    squares = jnp.sum(s[:, 2 * FF :], axis=1, keepdims=True)
    inverse = lax.rsqrt(squares / D + EPSILON)
    gate = s[:, :FF] * inverse
    up = s[:, FF : 2 * FF] * inverse
    out[...] = (gate / (1.0 + jnp.exp(-gate)) * up).astype(bf16)


def local(
    queries,
    own_latent,
    prefix_cache,
    block_home,
    row_prompt,
    chosen,
    value_up,
    out_weight,
    residual,
    norm_gain,
    gate_weight,
    up_weight,
):
    replica = lax.axis_index("dp")
    lane = lax.axis_index("tp")
    px, pz = replica // 4, replica % 4
    core = lane % 2
    i32 = jnp.int32
    where = jnp.stack([px, pz, core, lane]).astype(i32)

    q = queries.reshape(16, 16, KV).transpose(1, 0, 2).reshape(256, KV)
    q = jnp.concatenate([q, q[:, LAT:]], axis=1)
    own = jnp.concatenate([own_latent, own_latent[:, LAT:]], axis=1)
    qs = {0: q, **{k: send_y(q, k) for k in (1, 2, 3)}}

    picks, use = call(
        plan_kernel,
        "plan",
        [shape(CAP, 128, dtype=i32), shape(16, 64)],
        [where, row_prompt, block_home.reshape(4, 4, 128), row_prompt.reshape(1, 256), chosen.T],
        scalars=2,
    )

    sent = call(
        fetch_kernel,
        "fetch",
        [shape(8, 288, 128)] * 4,
        [where, picks, prefix_cache.reshape(16, BS, KV)],
        scalars=2,
    )
    got = [sent[0]] + [send_dp(sent[k], 0, k) for k in (1, 2, 3)]

    groups = call(regroup_kernel, "regroup", [shape(8, 288, 128)] * 4, [*got, use, *list(qs.values())[1:]], anys=4)
    arrived = {0: groups[0]}
    for k in (1, 3, 2):
        arrived[k] = send_dp(groups[k], 1, k)
    pieces = [groups[0], swap_core(groups[0])]
    *carry, done = attend(use, qs, 0, pieces, last=False)
    second, third = after(done, arrived[1], arrived[3])
    pieces = [second, swap_core(second), third, swap_core(third)]
    *carry, done = attend(use, qs, 1, pieces, carry, last=False)
    (fourth,) = after(done, arrived[2])
    pieces = [fourth, swap_core(fourth)]
    parts = []
    for k in (2, 1, 3, 0):
        (o,) = attend(use, {k: qs[k]}, 3, pieces, carry)
        parts.append(send_y(o, k) if k else o)
    per_head = merge(parts, q, own, value_up)

    near = [per_head] + [send_dp(per_head, 0, 4 - k) for k in (1, 2, 3)]
    near = jnp.concatenate(near, axis=0)
    far = [near] + [send_dp(near, 1, 4 - k) for k in (1, 2, 3)]
    keep, give = call(
        project_kernel,
        "project",
        [shape(2, 4, 16, 448, dtype=f32), shape(2, 4, 16, 448)],
        [where, *far, out_weight.T],
        scalars=1,
    )
    pair = (keep + swap_core(give).astype(f32)).astype(bf16)
    terms = [send_y(pair, k) for k in (1, 2, 3)]
    (half,) = call(
        join_kernel,
        "join",
        [shape(2, 4, 16, 448)],
        [where, pair, *terms, turn(residual.T).reshape(16, 16, 448)],
        scalars=1,
    )
    other = swap_core(half)
    stream, *sums = call(
        ffn_kernel,
        "ffn",
        [shape(16, 16, 448)] + [shape(4, 16, 2 * FF + 128)] * 4,
        [where, half, other, norm_gain.reshape(1, 448), gate_weight, up_weight],
        scalars=1,
        anys=2,
        limit=30,
        scratch_shapes=[pltpu.VMEM((448, FF), bf16)] * 2 + [pltpu.SemaphoreType.DMA(())] * 2,
    )
    got = [sums[0]] + [send_dp(sums[k], 0, k) for k in (2, 1, 3)]
    sums = call(fold_kernel, "fold", [shape(16, 2 * FF + 128)] * 4, got)
    got = [sums[0]] + [send_dp(sums[k], 1, k) for k in (2, 1, 3)]
    (hidden,) = call(finish_kernel, "finish", [shape(16, FF)], got)
    return (turn(stream.reshape(256, 448)).T, hidden)


def solution(mesh):
    placed = (
        P("dp", "tp"),
        P("dp", None),
        P(("dp", "tp"), None),
        P(),
        P(),
        P(),
        P("tp", None, None),
        P("tp", "dp"),
        P(None, "dp"),
        P("dp"),
        P("dp", "tp"),
        P("dp", "tp"),
    )
    return jax.shard_map(
        local, mesh=mesh, in_specs=placed, out_specs=(P(None, "dp"), P("dp", "tp")), check_vma=False
    )
```

```python
import functools
import math

import jax
import jax.numpy as jnp
from jax import lax
from jax.experimental import pallas as pl
from jax.experimental.pallas import tpu as pltpu
from jax.sharding import PartitionSpec as P

D = 7168
LAT = 512
ROPE = 64
QK_NOPE = 128
CAP = 2
PB = 512
BS = 64
KV = LAT + ROPE
EPSILON = 1e-06
FF = 2304
SCALE = 1.0 / math.sqrt(QK_NOPE + ROPE)
SCALE2 = SCALE / math.log(2.0)
NEG = -1e30
f32 = jnp.float32
bf16 = jnp.bfloat16


def send(x, axis, to, n):
    return lax.ppermute(x, axis, [(i, to(i)) for i in range(n)])


def swap_core(x):
    return send(x, "tp", lambda i: i ^ 1, 8)


def send_y(x, k):
    return send(x, "tp", lambda i: i ^ (2 * k), 8)


def send_dp(x, stage, k):
    pairs = []
    for i in range(128):
        dp, tp = i // 8, i % 8
        if tp % 2 == stage:
            to = ((dp // 4 + k) % 4) * 4 + dp % 4
        else:
            to = (dp // 4) * 4 + (dp % 4 + k) % 4
        pairs.append((i, to * 8 + tp))
    return lax.ppermute(x, ("dp", "tp"), pairs)


VMEM = pl.BlockSpec(memory_space=pltpu.VMEM)
SMEM = pl.BlockSpec(memory_space=pltpu.SMEM)
ANY = pl.BlockSpec(memory_space=pl.ANY)


def call(kernel, name, outs, ins, scalars=0, anys=0, limit=20, **kw):
    return pl.pallas_call(
        kernel,
        out_shape=outs,
        in_specs=[SMEM] * scalars + [VMEM] * (len(ins) - scalars - anys) + [ANY] * anys,
        out_specs=[VMEM] * len(outs),
        compiler_params=pltpu.CompilerParams(vmem_limit_bytes=limit * 1024 * 1024),
        name=name,
        **kw,
    )(*ins)


def shape(*dims, dtype=bf16):
    return jax.ShapeDtypeStruct(dims, dtype)


def place_of(where, ka, kb):
    px, pz, core = where[0], where[1], where[2]
    kx = jnp.where(core == 0, ka, kb)
    kz = jnp.where(core == 0, kb, ka)
    return ((px + kx) % 4) * 4 + (pz + kz) % 4


def plan_kernel(where, home_ref, prompt_ref, chosen_ref, picks_ref):
    px, pz, lane = where[0], where[1], where[3]
    replica = px * 4 + pz
    i32 = jnp.int32
    home = home_ref[...].reshape(16, 128)
    ids = lax.broadcasted_iota(i32, (16, 128), 0) * 128 + lax.broadcasted_iota(i32, (16, 128), 1)
    chosen = chosen_ref[...]
    wanted = chosen + prompt_ref[...] * PB
    asked = []
    for slot in range(16):
        found = home == (replica * 8 + lane) * 16 + slot
        block = jnp.sum(jnp.where(found, ids, 0), axis=(0, 1), keepdims=True)
        asked.append(jnp.max(jnp.where(wanted == block, 1.0, 0.0), axis=0, keepdims=True))
    asked = jnp.concatenate(asked, axis=0).astype(bf16)
    row = lax.broadcasted_iota(i32, (256, 128), 0)
    owner = lax.broadcasted_iota(i32, (256, 128), 1)
    owns = jnp.where(row // 16 == owner, 1.0, 0.0).astype(bf16)
    needed = jnp.dot(asked, owns, preferred_element_type=f32) > 0.5
    flag = jnp.where(needed, 1.0, 0.0)
    slot = lax.broadcasted_iota(i32, (16, 128), 0)
    low = lax.broadcasted_iota(i32, (16, 16), 0) > lax.broadcasted_iota(i32, (16, 16), 1)
    low = jnp.where(low, 1.0, 0.0).astype(bf16)
    before = jnp.dot(low, flag.astype(bf16), preferred_element_type=f32)
    for rank in range(CAP):
        pick = needed & (before > rank - 0.5) & (before < rank + 0.5)
        picks_ref[rank : rank + 1] = jnp.sum(jnp.where(pick, slot, 0), axis=0, keepdims=True)


def use_kernel(where, prompts, home_ref, chosen_ref, _, use_ref):
    px, pz, core, lane = where[0], where[1], where[2], where[3]
    replica = px * 4 + pz
    i32 = jnp.int32
    chosen = chosen_ref[...]
    mine = pltpu.roll(chosen, (256 - replica * 16) % 256, 1)[:, :128]
    mine = jnp.concatenate([mine.astype(f32), jnp.zeros((96, 128), f32)], axis=0).T[:16]
    block = lax.broadcasted_iota(i32, (16, PB), 1).astype(f32)
    uses = jnp.zeros((16, PB), f32)
    for t in range(32):
        uses = jnp.where(mine[:, t : t + 1] == block, 1.0, uses)
    need = jnp.max(uses, axis=0, keepdims=True) > 0.5
    here = home_ref[prompts[replica * 16]]
    here = jnp.concatenate([here[i : i + 1] for i in range(4)], axis=1)
    holder = here // 16
    live = jnp.where(need, here, -1).astype(f32)
    column = jnp.broadcast_to(live, (128, PB)).T[:, :1].astype(i32)
    fewer = (column // 16 == holder) & (column < here) & (column >= 0)
    rank = jnp.sum(jnp.where(fewer, 1, 0), axis=0, keepdims=True)
    key = jnp.where(need, holder * CAP + rank, -1)
    at = lax.broadcasted_iota(i32, (64, PB), 0)
    piece, ka, place = at // 8, (at // 2) % 4, at % 2
    sib = jnp.where((piece == 1) | (piece >= 5), 1, 0)
    kb = jnp.where(piece < 2, 0, (piece + 1) % 3 + 1)
    from_core = core ^ sib
    kx = jnp.where(from_core == 0, ka, kb)
    kz = jnp.where(from_core == 0, kb, ka)
    dev = (((px + 4 - kx) % 4) * 4 + (pz + 4 - kz) % 4) * 8 + lane - core + from_core
    hit = jnp.where(dev * CAP + place == key, 1.0, 0.0).astype(bf16)
    use = lax.dot_general(
        uses.astype(bf16), hit, (((1,), (1,)), ((), ())), preferred_element_type=f32
    )
    use_ref[...] = use.astype(bf16)


def fetch_kernel(where, picks, tokens, *outs):
    for ka in range(4):
        for kb in range(4):
            dest = place_of(where, ka, kb)
            for rank in range(CAP):
                pick = picks[rank, dest]
                out = outs[ka]
                at = kb * CAP + rank
                for c in range(4):
                    out[at, c * BS : (c + 1) * BS, :] = tokens[pick, :, c * 128 : (c + 1) * 128]
                rope = tokens[pick, :, LAT:KV]
                out[at, 4 * BS :, :] = jnp.concatenate([rope[:32], rope[32:]], axis=1)


def ask_kernel(queries, own, _, q_ref, own_ref):
    for head in range(16):
        x = queries[:, head * KV : (head + 1) * KV]
        rows = slice(head * 16, (head + 1) * 16)
        q_ref[rows, :LAT] = x[:, :LAT]
        q_ref[rows, LAT:] = jnp.concatenate([x[:, LAT:], x[:, LAT:]], axis=1)
    x = own[...]
    own_ref[:, :LAT] = x[:, :LAT]
    own_ref[:, LAT:] = jnp.concatenate([x[:, LAT:], x[:, LAT:]], axis=1)


def regroup_kernel(*refs):
    refs = refs[:4] + refs[8:]
    for ka in range(4):
        for kb in range(4):
            refs[4 + kb][ka * CAP : (ka + 1) * CAP] = refs[ka][kb * CAP : (kb + 1) * CAP]


def after_kernel(_, *refs):
    count = len(refs) // 2
    for i in range(count):
        refs[count + i][...] = refs[i][...]


def after(first, *blocks):
    return call(after_kernel, "after", [shape(8, 288, 128)] * len(blocks), [first, *blocks])


def half_latent(refs, half):
    rows = []
    for ref in refs:
        parts = [
            ref[:, c * BS + half * 32 : c * BS + half * 32 + 32, :].reshape(-1, 128)
            for c in range(4)
        ]
        rows.append(jnp.concatenate(parts, axis=1))
    return jnp.concatenate(rows, axis=0)


def half_rope(refs, half):
    rope = jnp.concatenate(
        [ref[:, 4 * BS : 4 * BS + 32, :].reshape(-1, 128) for ref in refs], axis=0
    )
    lane = lax.broadcasted_iota(jnp.int32, rope.shape, 1)
    keep = (lane < ROPE) if half == 0 else (lane >= ROPE)
    return jnp.where(keep, rope, jnp.zeros_like(rope))


def attend_kernel(first, sizes, chips, resume, last, *refs):
    groups, count = len(sizes), sum(sizes)
    use_ref, refs = refs[0], refs[1:]
    qs, refs = dict(zip(chips, refs)), refs[len(chips) :]
    pieces, refs = refs[:count], refs[count:]
    if resume:
        (acc_in, stat_in), refs = refs[:2], refs[2:]
    m_rows = 256
    members, biases = [], []
    for g, size in enumerate(sizes):
        at = sum(sizes[:g])
        members.append(pieces[at : at + size])
        slot = lax.broadcasted_iota(jnp.int32, (64, size * 512), 0)
        token = lax.broadcasted_iota(jnp.int32, (64, size * 512), 1)
        spread = (token // 32) % (8 * size) + 8 * (first + at) == slot
        spread = spread.astype(f32).astype(bf16)
        used = jnp.dot(use_ref[...], spread, preferred_element_type=f32)
        biases.append((used - 1.0) * -NEG)

    def values(g):
        return jnp.concatenate([half_latent(members[g], h) for h in range(2)], axis=0)

    def scores(chip, g):
        ropes = jnp.concatenate([half_rope(members[g], h) for h in range(2)], axis=0)
        keys = jnp.concatenate([values(g), ropes], axis=1)
        s = lax.dot_general(
            qs[chip][...], keys, (((1,), (1,)), ((), ())), preferred_element_type=f32
        )
        n = s.shape[1]
        return (s.reshape(m_rows // 16, 16, n) + biases[g][None]).reshape(m_rows, n)

    steps = [(chip, g) for chip in chips for g in range(groups)]
    s = scores(*steps[0])
    for i, (chip, g) in enumerate(steps):
        ahead = scores(*steps[i + 1]) if i + 1 < len(steps) else None
        if g == 0:
            top = total = acc = None
            if resume:
                top, total = stat_in[chip, :, 0:1], stat_in[chip, :, 64:65]
                acc = acc_in[chip]
        high = jnp.max(s, axis=1, keepdims=True)
        new = high if top is None else jnp.maximum(top, high)
        p = jnp.exp2((s - new) * SCALE2)
        part = jnp.sum(p, axis=1, keepdims=True)
        o = jnp.dot(p.astype(bf16), values(g), preferred_element_type=f32)
        if top is None:
            acc, total = o, part
        else:
            fade = jnp.exp2((top - new) * SCALE2)
            acc, total = acc * fade + o, total * fade + part
        top, s = new, ahead
        if g == groups - 1 and last:
            finish_heads(acc, top, total, refs[chips.index(chip)])
        elif g == groups - 1:
            lane = lax.broadcasted_iota(jnp.int32, (m_rows, 128), 1)
            refs[0][chip] = acc
            refs[1][chip] = jnp.where(lane < 64, top, total)
    if not last:
        refs[2][...] = jnp.zeros((8, 128), f32)


def finish_heads(acc, top, total, out_ref):
    m_rows = 256
    out_ref[:m_rows] = (acc / total).astype(bf16)
    lse = top * SCALE + jnp.log(total)
    hi = lse.astype(bf16).astype(f32)
    mid = (lse - hi).astype(bf16).astype(f32)
    low = lse - hi - mid
    lane = lax.broadcasted_iota(jnp.int32, (m_rows, 128), 1)
    stats = jnp.where(lane == 0, hi, jnp.where(lane == 1, mid, jnp.where(lane == 2, low, 0.0)))
    stats = stats.T[:16]
    out_ref[m_rows:] = jnp.concatenate([stats, jnp.zeros_like(stats)], axis=1).astype(bf16)


def attend(use, qs, first, sizes, pieces, carry=(), last=True):
    if last:
        outs = [shape(256 + 16, LAT)] * len(qs)
    else:
        outs = [shape(4, 256, LAT, dtype=f32), shape(4, 256, 128, dtype=f32)]
        outs.append(shape(8, 128, dtype=f32))
    return call(
        functools.partial(attend_kernel, first, sizes, list(qs), bool(carry), last),
        "attend",
        outs,
        [use, *qs.values(), *pieces, *carry],
        limit=16,
    )


def merge_kernel(o0, o1, o2, o3, q_ref, own_ref, up_ref, out_ref):
    heads, rows = 16, 16
    own = own_ref[...].astype(f32)
    q = q_ref[...].astype(f32).reshape(heads, rows, 640)
    lane = lax.broadcasted_iota(jnp.int32, (rows, 640), 1)
    key = jnp.where(lane < KV, own, 0.0)
    s_own = jnp.sum(q * key[None], axis=2, keepdims=True).reshape(heads * rows, 1) * SCALE
    lses = []
    for o in (o0, o1, o2, o3):
        row = jnp.sum(o[256:, :256].astype(f32), axis=0, keepdims=True)
        lses.append(jnp.broadcast_to(row, (128, 256)).T[:, :1])
    top = s_own
    for v in lses:
        top = jnp.maximum(top, v)
    e_own = jnp.exp(s_own - top)
    es = [jnp.exp(v - top) for v in lses]
    den = e_own + ((es[0] + es[1]) + (es[2] + es[3]))
    mix = (e_own / den).reshape(heads, rows, 1) * own[None, :, :LAT]
    mix = mix.reshape(heads * rows, LAT)
    for o, e in zip((o0, o1, o2, o3), es):
        mix = mix + (e / den) * o[:256].astype(f32)
    mix = mix.astype(bf16)
    for h in range(heads):
        out_ref[:, h * 128 : (h + 1) * 128] = jnp.dot(
            mix[h * rows : (h + 1) * rows], up_ref[h], preferred_element_type=f32
        ).astype(bf16)


def merge(parts, q, own, value_up):
    return pl.pallas_call(
        merge_kernel,
        out_shape=jax.ShapeDtypeStruct((16, 2048), bf16),
        in_specs=[pl.BlockSpec(memory_space=pltpu.VMEM)] * 7,
        out_specs=pl.BlockSpec(memory_space=pltpu.VMEM),
        compiler_params=pltpu.CompilerParams(vmem_limit_bytes=24 * 1024 * 1024),
        name="merge",
    )(*parts, q, own, value_up)


def project_kernel(where, p0, p1, p2, p3, weight, keep_ref, give_ref):
    core = where[2]
    rows = jnp.concatenate([p0[...], p1[...], p2[...], p3[...]], axis=0)
    full = lax.dot_general(
        rows, weight[...], (((1,), (1,)), ((), ())), preferred_element_type=f32
    ).reshape(4, 4, 16, 448)

    @pl.when(core == 0)
    def _():
        keep_ref[...] = full[:2]
        give_ref[...] = full[2:].astype(bf16)

    @pl.when(core == 1)
    def _():
        for i in range(2):
            keep_ref[i] = full[:, 2 + i]
            give_ref[i] = full[:, i].astype(bf16)


def join_kernel(where, pair, t1, t2, t3, residual, out):
    px, pz, core = where[0], where[1], where[2]
    for i in range(2):
        for kx in range(4):
            kz = core * 2 + i
            dp = ((px + kx) % 4) * 4 + (pz + kz) % 4
            attn = (pair[i, kx].astype(f32) + t1[i, kx].astype(f32)) + (
                t2[i, kx].astype(f32) + t3[i, kx].astype(f32)
            )
            out[i, kx] = (residual[dp].astype(f32) + attn).astype(bf16)


def ffn_kernel(where, half_ref, other_ref, gain_ref, wg_ref, wu_ref, stream_ref, *outs):
    px, pz, core = where[0], where[1], where[2]
    half, other = half_ref[...].astype(f32), other_ref[...].astype(f32)
    rows = jnp.concatenate(
        [jnp.where(core == 0, half, other), jnp.where(core == 0, other, half)], axis=0
    )
    for kz in range(4):
        for kx in range(4):
            stream_ref[((px + kx) % 4) * 4 + (pz + kz) % 4] = rows[kz, kx].astype(bf16)
    turned = jnp.stack([rows[:, k] for k in range(4)], axis=0)
    wide = jnp.where(core == 0, rows, turned).reshape(256, 448)
    squares = jnp.sum(wide * wide, axis=1, keepdims=True)
    hi = squares.astype(bf16).astype(f32)
    lane = lax.broadcasted_iota(jnp.int32, (256, 128), 1)
    tail = jnp.where(lane == 0, hi, jnp.where(lane == 1, squares - hi, 0.0)).astype(bf16)
    scaled = (wide * gain_ref[...].astype(f32)).astype(bf16)
    gate = jnp.dot(scaled, wg_ref[...], preferred_element_type=f32).astype(bf16)
    gate = gate.reshape(4, 4, 16, FF)
    tail = tail.reshape(4, 4, 16, 128)
    for k in range(4):
        outs[k][:, :, :FF] = gate[:, k]
        outs[k][:, :, 2 * FF :] = tail[:, k]
    up = jnp.dot(scaled, wu_ref[...], preferred_element_type=f32).astype(bf16)
    up = up.reshape(4, 4, 16, FF)
    for k in range(4):
        outs[k][:, :, FF : 2 * FF] = up[:, k]


def turn_kernel(x, out):
    out[...] = x[...].astype(f32).T.astype(bf16)


def turn(x):
    return call(turn_kernel, "turn", [shape(x.shape[1], x.shape[0])], [x])[0]


def sum4(refs, at):
    a, b, c, d = (ref[at].astype(f32) for ref in refs)
    return (a + b) + (c + d)


def fold_kernel(*refs):
    for kb in range(4):
        s = sum4(refs[:4], kb)
        refs[4 + kb][:, : 2 * FF] = s[:, : 2 * FF].astype(bf16)
        squares = jnp.sum(s[:, 2 * FF :], axis=1, keepdims=True)
        hi = squares.astype(bf16).astype(f32)
        lane = lax.broadcasted_iota(jnp.int32, (16, 128), 1)
        tail = jnp.where(lane == 0, hi, jnp.where(lane == 1, squares - hi, 0.0))
        refs[4 + kb][:, 2 * FF :] = tail.astype(bf16)


def finish_kernel(r0, r1, r2, r3, out):
    s = sum4((r0, r1, r2, r3), ...)
    squares = jnp.sum(s[:, 2 * FF :], axis=1, keepdims=True)
    inverse = lax.rsqrt(squares / D + EPSILON)
    gate = s[:, :FF] * inverse
    up = s[:, FF : 2 * FF] * inverse
    out[...] = (gate / (1.0 + jnp.exp(-gate)) * up).astype(bf16)


def local(
    queries,
    own_latent,
    prefix_cache,
    block_home,
    row_prompt,
    chosen,
    value_up,
    out_weight,
    residual,
    norm_gain,
    gate_weight,
    up_weight,
):
    replica = lax.axis_index("dp")
    lane = lax.axis_index("tp")
    px, pz = replica // 4, replica % 4
    core = lane % 2
    i32 = jnp.int32
    where = jnp.stack([px, pz, core, lane]).astype(i32)

    homes = block_home.reshape(4, 4, 128)
    (picks,) = call(
        plan_kernel,
        "plan",
        [shape(CAP, 128, dtype=i32)],
        [where, homes, row_prompt.reshape(1, 256), chosen.T],
        scalars=1,
    )

    sent = call(
        fetch_kernel,
        "fetch",
        [shape(8, 288, 128)] * 4,
        [where, picks, prefix_cache.reshape(16, BS, KV)],
        scalars=2,
    )
    got = [sent[0]] + [send_dp(sent[k], 0, k) for k in (1, 2, 3)]

    (use,) = call(
        use_kernel,
        "use",
        [shape(16, 64)],
        [where, row_prompt, homes, chosen.T, sent[0]],
        scalars=2,
        anys=1,
    )

    q, own = call(
        ask_kernel,
        "ask",
        [shape(256, LAT + 128), shape(16, LAT + 128)],
        [queries, own_latent, sent[0]],
        anys=1,
    )
    qs = {0: q, **{k: send_y(q, k) for k in (1, 2, 3)}}

    groups = call(regroup_kernel, "regroup", [shape(8, 288, 128)] * 4, [*got, use, *list(qs.values())[1:]], anys=4)
    arrived = {0: groups[0]}
    for k in (1, 3, 2):
        arrived[k] = send_dp(groups[k], 1, k)
    pieces = [groups[0], swap_core(groups[0])]
    *carry, done = attend(use, qs, 0, (2,), pieces, last=False)
    far = after(done, arrived[1], arrived[2], arrived[3])
    far_other = [swap_core(v) for v in far]
    others = {k: qs[k] for k in (2, 1, 3)}
    *rest, done = attend(use, others, 2, (2, 1), far, carry, last=False)
    parts = []
    for k in others:
        (o,) = attend(use, {k: qs[k]}, 5, (2, 1), far_other, rest)
        parts.append(send_y(o, k))
    parts += attend(use, {0: q}, 2, (2, 2, 2), list(far) + far_other, carry)
    per_head = merge(parts, q, own, value_up)

    near = [per_head] + [send_dp(per_head, 0, 4 - k) for k in (1, 2, 3)]
    near = jnp.concatenate(near, axis=0)
    far = [near] + [send_dp(near, 1, 4 - k) for k in (1, 2, 3)]
    keep, give = call(
        project_kernel,
        "project",
        [shape(2, 4, 16, 448, dtype=f32), shape(2, 4, 16, 448)],
        [where, *far, out_weight.T],
        scalars=1,
    )
    pair = (keep + swap_core(give).astype(f32)).astype(bf16)
    terms = [send_y(pair, k) for k in (1, 2, 3)]
    (half,) = call(
        join_kernel,
        "join",
        [shape(2, 4, 16, 448)],
        [where, pair, *terms, turn(residual.T).reshape(16, 16, 448)],
        scalars=1,
    )
    other = swap_core(half)
    stream, *sums = call(
        ffn_kernel,
        "ffn",
        [shape(16, 16, 448)] + [shape(4, 16, 2 * FF + 128)] * 4,
        [where, half, other, norm_gain.reshape(1, 448), gate_weight, up_weight],
        scalars=1,
        limit=30,
    )
    got = [sums[0]] + [send_dp(sums[k], 0, k) for k in (2, 1, 3)]
    sums = call(fold_kernel, "fold", [shape(16, 2 * FF + 128)] * 4, got)
    got = [sums[0]] + [send_dp(sums[k], 1, k) for k in (2, 1, 3)]
    (hidden,) = call(finish_kernel, "finish", [shape(16, FF)], got)
    return (turn(stream.reshape(256, 448)).T, hidden)


def solution(mesh):
    placed = (
        P("dp", "tp"),
        P("dp", None),
        P(("dp", "tp"), None),
        P(),
        P(),
        P(),
        P("tp", None, None),
        P("tp", "dp"),
        P(None, "dp"),
        P("dp"),
        P("dp", "tp"),
        P("dp", "tp"),
    )
    return jax.shard_map(
        local, mesh=mesh, in_specs=placed, out_specs=(P(None, "dp"), P("dp", "tp")), check_vma=False
    )
```

```python
import functools
import math

import jax
import jax.numpy as jnp
from jax import lax
from jax.experimental import pallas as pl
from jax.experimental.pallas import tpu as pltpu
from jax.sharding import PartitionSpec as P

D = 7168
LAT = 512
ROPE = 64
QK_NOPE = 128
CAP = 2
PB = 512
BS = 64
KV = LAT + ROPE
EPSILON = 1e-06
FF = 2304
SCALE = 1.0 / math.sqrt(QK_NOPE + ROPE)
SCALE2 = SCALE / math.log(2.0)
NEG = -1e30
f32 = jnp.float32
bf16 = jnp.bfloat16


def send(x, axis, to, n):
    return lax.ppermute(x, axis, [(i, to(i)) for i in range(n)])


def swap_core(x):
    return send(x, "tp", lambda i: i ^ 1, 8)


def send_y(x, k):
    return send(x, "tp", lambda i: i ^ (2 * k), 8)


def send_dp(x, stage, k):
    pairs = []
    for i in range(128):
        dp, tp = i // 8, i % 8
        if tp % 2 == stage:
            to = ((dp // 4 + k) % 4) * 4 + dp % 4
        else:
            to = (dp // 4) * 4 + (dp % 4 + k) % 4
        pairs.append((i, to * 8 + tp))
    return lax.ppermute(x, ("dp", "tp"), pairs)


VMEM = pl.BlockSpec(memory_space=pltpu.VMEM)
SMEM = pl.BlockSpec(memory_space=pltpu.SMEM)
ANY = pl.BlockSpec(memory_space=pl.ANY)


def call(kernel, name, outs, ins, scalars=0, anys=0, limit=20, **kw):
    return pl.pallas_call(
        kernel,
        out_shape=outs,
        in_specs=[SMEM] * scalars + [VMEM] * (len(ins) - scalars - anys) + [ANY] * anys,
        out_specs=[VMEM] * len(outs),
        compiler_params=pltpu.CompilerParams(vmem_limit_bytes=limit * 1024 * 1024),
        name=name,
        **kw,
    )(*ins)


def shape(*dims, dtype=bf16):
    return jax.ShapeDtypeStruct(dims, dtype)


def place_of(where, ka, kb):
    px, pz, core = where[0], where[1], where[2]
    kx = jnp.where(core == 0, ka, kb)
    kz = jnp.where(core == 0, kb, ka)
    return ((px + kx) % 4) * 4 + (pz + kz) % 4


def plan_kernel(where, home_ref, prompt_ref, chosen_ref, picks_ref):
    px, pz, lane = where[0], where[1], where[3]
    replica = px * 4 + pz
    i32 = jnp.int32
    home = home_ref[...].reshape(16, 128)
    ids = lax.broadcasted_iota(i32, (16, 128), 0) * 128 + lax.broadcasted_iota(i32, (16, 128), 1)
    chosen = chosen_ref[...]
    wanted = chosen + prompt_ref[...] * PB
    asked = []
    for slot in range(16):
        found = home == (replica * 8 + lane) * 16 + slot
        block = jnp.sum(jnp.where(found, ids, 0), axis=(0, 1), keepdims=True)
        asked.append(jnp.max(jnp.where(wanted == block, 1.0, 0.0), axis=0, keepdims=True))
    asked = jnp.concatenate(asked, axis=0).astype(bf16)
    row = lax.broadcasted_iota(i32, (256, 128), 0)
    owner = lax.broadcasted_iota(i32, (256, 128), 1)
    owns = jnp.where(row // 16 == owner, 1.0, 0.0).astype(bf16)
    needed = jnp.dot(asked, owns, preferred_element_type=f32) > 0.5
    flag = jnp.where(needed, 1.0, 0.0)
    slot = lax.broadcasted_iota(i32, (16, 128), 0)
    low = lax.broadcasted_iota(i32, (16, 16), 0) > lax.broadcasted_iota(i32, (16, 16), 1)
    low = jnp.where(low, 1.0, 0.0).astype(bf16)
    before = jnp.dot(low, flag.astype(bf16), preferred_element_type=f32)
    for rank in range(CAP):
        pick = needed & (before > rank - 0.5) & (before < rank + 0.5)
        picks_ref[rank : rank + 1] = jnp.sum(jnp.where(pick, slot, 0), axis=0, keepdims=True)


def use_kernel(where, prompts, home_ref, chosen_ref, _, use_ref):
    px, pz, core, lane = where[0], where[1], where[2], where[3]
    replica = px * 4 + pz
    i32 = jnp.int32
    chosen = chosen_ref[...]
    mine = pltpu.roll(chosen, (256 - replica * 16) % 256, 1)[:, :128]
    mine = jnp.concatenate([mine.astype(f32), jnp.zeros((96, 128), f32)], axis=0).T[:16]
    block = lax.broadcasted_iota(i32, (16, PB), 1).astype(f32)
    uses = jnp.zeros((16, PB), f32)
    for t in range(32):
        uses = jnp.where(mine[:, t : t + 1] == block, 1.0, uses)
    need = jnp.max(uses, axis=0, keepdims=True) > 0.5
    here = home_ref[prompts[replica * 16]]
    here = jnp.concatenate([here[i : i + 1] for i in range(4)], axis=1)
    holder = here // 16
    live = jnp.where(need, here, -1).astype(f32)
    column = jnp.broadcast_to(live, (128, PB)).T[:, :1].astype(i32)
    fewer = (column // 16 == holder) & (column < here) & (column >= 0)
    rank = jnp.sum(jnp.where(fewer, 1, 0), axis=0, keepdims=True)
    key = jnp.where(need, holder * CAP + rank, -1)
    at = lax.broadcasted_iota(i32, (64, PB), 0)
    piece, ka, place = at // 8, (at // 2) % 4, at % 2
    sib = jnp.where((piece == 1) | (piece >= 5), 1, 0)
    kb = jnp.where(piece < 2, 0, (piece + 1) % 3 + 1)
    from_core = core ^ sib
    kx = jnp.where(from_core == 0, ka, kb)
    kz = jnp.where(from_core == 0, kb, ka)
    dev = (((px + 4 - kx) % 4) * 4 + (pz + 4 - kz) % 4) * 8 + lane - core + from_core
    hit = jnp.where(dev * CAP + place == key, 1.0, 0.0).astype(bf16)
    use = lax.dot_general(
        uses.astype(bf16), hit, (((1,), (1,)), ((), ())), preferred_element_type=f32
    )
    use_ref[...] = use.astype(bf16)


def fetch_kernel(where, picks, tokens, *outs):
    for ka in range(4):
        for kb in range(4):
            dest = place_of(where, ka, kb)
            for rank in range(CAP):
                pick = picks[rank, dest]
                out = outs[ka]
                at = kb * CAP + rank
                for c in range(4):
                    out[at, c * BS : (c + 1) * BS, :] = tokens[pick, :, c * 128 : (c + 1) * 128]
                rope = tokens[pick, :, LAT:KV]
                out[at, 4 * BS :, :] = jnp.concatenate([rope[:32], rope[32:]], axis=1)


def ask_kernel(queries, own, _, q_ref, own_ref):
    for head in range(16):
        x = queries[:, head * KV : (head + 1) * KV]
        rows = slice(head * 16, (head + 1) * 16)
        q_ref[rows, :LAT] = x[:, :LAT]
        q_ref[rows, LAT:] = jnp.concatenate([x[:, LAT:], x[:, LAT:]], axis=1)
    x = own[...]
    own_ref[:, :LAT] = x[:, :LAT]
    own_ref[:, LAT:] = jnp.concatenate([x[:, LAT:], x[:, LAT:]], axis=1)


def regroup_kernel(*refs):
    refs = refs[:4] + refs[6:]
    for ka in range(4):
        for kb in range(4):
            refs[4 + kb][ka * CAP : (ka + 1) * CAP] = refs[ka][kb * CAP : (kb + 1) * CAP]


def after_kernel(_, *refs):
    count = len(refs) // 2
    for i in range(count):
        refs[count + i][...] = refs[i][...]


def after(first, *blocks):
    return call(after_kernel, "after", [shape(8, 288, 128)] * len(blocks), [first, *blocks])


def half_latent(refs, half):
    rows = []
    for ref in refs:
        parts = [
            ref[:, c * BS + half * 32 : c * BS + half * 32 + 32, :].reshape(-1, 128)
            for c in range(4)
        ]
        rows.append(jnp.concatenate(parts, axis=1))
    return jnp.concatenate(rows, axis=0)


def half_rope(refs, half):
    rope = jnp.concatenate(
        [ref[:, 4 * BS : 4 * BS + 32, :].reshape(-1, 128) for ref in refs], axis=0
    )
    lane = lax.broadcasted_iota(jnp.int32, rope.shape, 1)
    keep = (lane < ROPE) if half == 0 else (lane >= ROPE)
    return jnp.where(keep, rope, jnp.zeros_like(rope))


def attend_kernel(first, sizes, chips, resume, last, *refs):
    groups, count = len(sizes), sum(sizes)
    use_ref, refs = refs[0], refs[1:]
    qs, refs = dict(zip(chips, refs)), refs[len(chips) :]
    pieces, refs = refs[:count], refs[count:]
    if resume:
        (acc_in, stat_in), refs = refs[:2], refs[2:]
    m_rows = 256
    members, biases = [], []
    for g, size in enumerate(sizes):
        at = sum(sizes[:g])
        members.append(pieces[at : at + size])
        slot = lax.broadcasted_iota(jnp.int32, (64, size * 512), 0)
        token = lax.broadcasted_iota(jnp.int32, (64, size * 512), 1)
        spread = (token // 32) % (8 * size) + 8 * (first + at) == slot
        spread = spread.astype(f32).astype(bf16)
        used = jnp.dot(use_ref[...], spread, preferred_element_type=f32)
        biases.append((used - 1.0) * -NEG)

    def values(g):
        return jnp.concatenate([half_latent(members[g], h) for h in range(2)], axis=0)

    def scores(chip, g):
        ropes = jnp.concatenate([half_rope(members[g], h) for h in range(2)], axis=0)
        keys = jnp.concatenate([values(g), ropes], axis=1)
        s = lax.dot_general(
            qs[chip][...], keys, (((1,), (1,)), ((), ())), preferred_element_type=f32
        )
        n = s.shape[1]
        return (s.reshape(m_rows // 16, 16, n) + biases[g][None]).reshape(m_rows, n)

    steps = [(chip, g) for chip in chips for g in range(groups)]
    s = scores(*steps[0])
    for i, (chip, g) in enumerate(steps):
        ahead = scores(*steps[i + 1]) if i + 1 < len(steps) else None
        if g == 0:
            top = total = acc = None
            if resume:
                top, total = stat_in[chip, :, 0:1], stat_in[chip, :, 64:65]
                acc = acc_in[chip]
        high = jnp.max(s, axis=1, keepdims=True)
        new = high if top is None else jnp.maximum(top, high)
        p = jnp.exp2((s - new) * SCALE2)
        part = jnp.sum(p, axis=1, keepdims=True)
        o = jnp.dot(p.astype(bf16), values(g), preferred_element_type=f32)
        if top is None:
            acc, total = o, part
        else:
            fade = jnp.exp2((top - new) * SCALE2)
            acc, total = acc * fade + o, total * fade + part
        top, s = new, ahead
        if g == groups - 1 and last:
            finish_heads(acc, top, total, refs[chips.index(chip)])
        elif g == groups - 1:
            lane = lax.broadcasted_iota(jnp.int32, (m_rows, 128), 1)
            refs[0][chip] = acc
            refs[1][chip] = jnp.where(lane < 64, top, total)
    if not last:
        refs[2][...] = jnp.zeros((8, 128), f32)


def finish_heads(acc, top, total, out_ref):
    m_rows = 256
    out_ref[:m_rows] = (acc / total).astype(bf16)
    lse = top * SCALE + jnp.log(total)
    hi = lse.astype(bf16).astype(f32)
    mid = (lse - hi).astype(bf16).astype(f32)
    low = lse - hi - mid
    lane = lax.broadcasted_iota(jnp.int32, (m_rows, 128), 1)
    stats = jnp.where(lane == 0, hi, jnp.where(lane == 1, mid, jnp.where(lane == 2, low, 0.0)))
    stats = stats.T[:16]
    out_ref[m_rows:] = jnp.concatenate([stats, jnp.zeros_like(stats)], axis=1).astype(bf16)


def attend(use, qs, first, sizes, pieces, carry=(), last=True):
    if last:
        outs = [shape(256 + 16, LAT)] * len(qs)
    else:
        outs = [shape(4, 256, LAT, dtype=f32), shape(4, 256, 128, dtype=f32)]
        outs.append(shape(8, 128, dtype=f32))
    return call(
        functools.partial(attend_kernel, first, sizes, list(qs), bool(carry), last),
        "attend",
        outs,
        [use, *qs.values(), *pieces, *carry],
        limit=16,
    )


def merge_kernel(o0, o1, o2, o3, q_ref, own_ref, up_ref, out_ref):
    heads, rows = 16, 16
    own = own_ref[...].astype(f32)
    q = q_ref[...].astype(f32).reshape(heads, rows, 640)
    lane = lax.broadcasted_iota(jnp.int32, (rows, 640), 1)
    key = jnp.where(lane < KV, own, 0.0)
    s_own = jnp.sum(q * key[None], axis=2, keepdims=True).reshape(heads * rows, 1) * SCALE
    lses = []
    for o in (o0, o1, o2, o3):
        row = jnp.sum(o[256:, :256].astype(f32), axis=0, keepdims=True)
        lses.append(jnp.broadcast_to(row, (128, 256)).T[:, :1])
    top = s_own
    for v in lses:
        top = jnp.maximum(top, v)
    e_own = jnp.exp(s_own - top)
    es = [jnp.exp(v - top) for v in lses]
    den = e_own + ((es[0] + es[1]) + (es[2] + es[3]))
    mix = (e_own / den).reshape(heads, rows, 1) * own[None, :, :LAT]
    mix = mix.reshape(heads * rows, LAT)
    for o, e in zip((o0, o1, o2, o3), es):
        mix = mix + (e / den) * o[:256].astype(f32)
    mix = mix.astype(bf16)
    for h in range(heads):
        out_ref[:, h * 128 : (h + 1) * 128] = jnp.dot(
            mix[h * rows : (h + 1) * rows], up_ref[h], preferred_element_type=f32
        ).astype(bf16)


def merge(parts, q, own, value_up):
    return pl.pallas_call(
        merge_kernel,
        out_shape=jax.ShapeDtypeStruct((16, 2048), bf16),
        in_specs=[pl.BlockSpec(memory_space=pltpu.VMEM)] * 7,
        out_specs=pl.BlockSpec(memory_space=pltpu.VMEM),
        compiler_params=pltpu.CompilerParams(vmem_limit_bytes=24 * 1024 * 1024),
        name="merge",
    )(*parts, q, own, value_up)


def project_kernel(where, p0, p1, p2, p3, weight, keep_ref, give_ref):
    core = where[2]
    rows = jnp.concatenate([p0[...], p1[...], p2[...], p3[...]], axis=0)
    full = lax.dot_general(
        rows, weight[...], (((1,), (1,)), ((), ())), preferred_element_type=f32
    ).reshape(4, 4, 16, 448)

    @pl.when(core == 0)
    def _():
        keep_ref[...] = full[:2]
        give_ref[...] = full[2:].astype(bf16)

    @pl.when(core == 1)
    def _():
        for i in range(2):
            keep_ref[i] = full[:, 2 + i]
            give_ref[i] = full[:, i].astype(bf16)


def join_kernel(where, pair, t1, t2, t3, residual, out):
    px, pz, core = where[0], where[1], where[2]
    for i in range(2):
        for kx in range(4):
            kz = core * 2 + i
            dp = ((px + kx) % 4) * 4 + (pz + kz) % 4
            attn = (pair[i, kx].astype(f32) + t1[i, kx].astype(f32)) + (
                t2[i, kx].astype(f32) + t3[i, kx].astype(f32)
            )
            out[i, kx] = (residual[dp].astype(f32) + attn).astype(bf16)


def ffn_kernel(where, half_ref, other_ref, gain_ref, wg_ref, wu_ref, stream_ref, *outs):
    px, pz, core = where[0], where[1], where[2]
    half, other = half_ref[...].astype(f32), other_ref[...].astype(f32)
    rows = jnp.concatenate(
        [jnp.where(core == 0, half, other), jnp.where(core == 0, other, half)], axis=0
    )
    for kz in range(4):
        for kx in range(4):
            stream_ref[((px + kx) % 4) * 4 + (pz + kz) % 4] = rows[kz, kx].astype(bf16)
    turned = jnp.stack([rows[:, k] for k in range(4)], axis=0)
    wide = jnp.where(core == 0, rows, turned).reshape(256, 448)
    squares = jnp.sum(wide * wide, axis=1, keepdims=True)
    hi = squares.astype(bf16).astype(f32)
    lane = lax.broadcasted_iota(jnp.int32, (256, 128), 1)
    tail = jnp.where(lane == 0, hi, jnp.where(lane == 1, squares - hi, 0.0)).astype(bf16)
    scaled = (wide * gain_ref[...].astype(f32)).astype(bf16)
    gate = jnp.dot(scaled, wg_ref[...], preferred_element_type=f32).astype(bf16)
    gate = gate.reshape(4, 4, 16, FF)
    tail = tail.reshape(4, 4, 16, 128)
    for k in range(4):
        outs[k][:, :, :FF] = gate[:, k]
        outs[k][:, :, 2 * FF :] = tail[:, k]
    up = jnp.dot(scaled, wu_ref[...], preferred_element_type=f32).astype(bf16)
    up = up.reshape(4, 4, 16, FF)
    for k in range(4):
        outs[k][:, :, FF : 2 * FF] = up[:, k]


def turn_kernel(x, out):
    out[...] = x[...].astype(f32).T.astype(bf16)


def turn(x):
    return call(turn_kernel, "turn", [shape(x.shape[1], x.shape[0])], [x])[0]


def sum4(refs, at):
    a, b, c, d = (ref[at].astype(f32) for ref in refs)
    return (a + b) + (c + d)


def fold_kernel(*refs):
    for kb in range(4):
        s = sum4(refs[:4], kb)
        refs[4 + kb][:, : 2 * FF] = s[:, : 2 * FF].astype(bf16)
        squares = jnp.sum(s[:, 2 * FF :], axis=1, keepdims=True)
        hi = squares.astype(bf16).astype(f32)
        lane = lax.broadcasted_iota(jnp.int32, (16, 128), 1)
        tail = jnp.where(lane == 0, hi, jnp.where(lane == 1, squares - hi, 0.0))
        refs[4 + kb][:, 2 * FF :] = tail.astype(bf16)


def finish_kernel(r0, r1, r2, r3, out):
    s = sum4((r0, r1, r2, r3), ...)
    squares = jnp.sum(s[:, 2 * FF :], axis=1, keepdims=True)
    inverse = lax.rsqrt(squares / D + EPSILON)
    gate = s[:, :FF] * inverse
    up = s[:, FF : 2 * FF] * inverse
    out[...] = (gate / (1.0 + jnp.exp(-gate)) * up).astype(bf16)


def local(
    queries,
    own_latent,
    prefix_cache,
    block_home,
    row_prompt,
    chosen,
    value_up,
    out_weight,
    residual,
    norm_gain,
    gate_weight,
    up_weight,
):
    replica = lax.axis_index("dp")
    lane = lax.axis_index("tp")
    px, pz = replica // 4, replica % 4
    core = lane % 2
    i32 = jnp.int32
    where = jnp.stack([px, pz, core, lane]).astype(i32)

    homes = block_home.reshape(4, 4, 128)
    (picks,) = call(
        plan_kernel,
        "plan",
        [shape(CAP, 128, dtype=i32)],
        [where, homes, row_prompt.reshape(1, 256), chosen.T],
        scalars=1,
    )

    sent = call(
        fetch_kernel,
        "fetch",
        [shape(8, 288, 128)] * 4,
        [where, picks, prefix_cache.reshape(16, BS, KV)],
        scalars=2,
    )
    got = [sent[0]] + [send_dp(sent[k], 0, k) for k in (1, 2, 3)]

    (use,) = call(
        use_kernel,
        "use",
        [shape(16, 64)],
        [where, row_prompt, homes, chosen.T, sent[0]],
        scalars=2,
        anys=1,
    )

    q, own = call(
        ask_kernel,
        "ask",
        [shape(256, LAT + 128), shape(16, LAT + 128)],
        [queries, own_latent, sent[0]],
        anys=1,
    )
    qs = {0: q, **{k: send_y(q, k) for k in (1, 2, 3)}}

    groups = call(regroup_kernel, "regroup", [shape(8, 288, 128)] * 4, [*got, use, qs[2]], anys=2)
    arrived = {0: groups[0]}
    for k in (1, 3, 2):
        arrived[k] = send_dp(groups[k], 1, k)
    pieces = [groups[0], swap_core(groups[0])]
    *carry, done = attend(use, qs, 0, (2,), pieces, last=False)
    far = after(done, arrived[1], arrived[2], arrived[3])
    far_other = [swap_core(v) for v in far]
    others = {k: qs[k] for k in (2, 1, 3)}
    *rest, done = attend(use, others, 2, (2, 1), far, carry, last=False)
    parts = []
    for k in others:
        (o,) = attend(use, {k: qs[k]}, 5, (2, 1), far_other, rest)
        parts.append(send_y(o, k))
    parts += attend(use, {0: q}, 2, (2, 2, 2), list(far) + far_other, carry)
    per_head = merge(parts, q, own, value_up)

    near = [per_head] + [send_dp(per_head, 0, 4 - k) for k in (1, 2, 3)]
    near = jnp.concatenate(near, axis=0)
    far = [near] + [send_dp(near, 1, 4 - k) for k in (1, 2, 3)]
    keep, give = call(
        project_kernel,
        "project",
        [shape(2, 4, 16, 448, dtype=f32), shape(2, 4, 16, 448)],
        [where, *far, out_weight.T],
        scalars=1,
    )
    pair = (keep + swap_core(give).astype(f32)).astype(bf16)
    terms = [send_y(pair, k) for k in (1, 2, 3)]
    (half,) = call(
        join_kernel,
        "join",
        [shape(2, 4, 16, 448)],
        [where, pair, *terms, turn(residual.T).reshape(16, 16, 448)],
        scalars=1,
    )
    other = swap_core(half)
    stream, *sums = call(
        ffn_kernel,
        "ffn",
        [shape(16, 16, 448)] + [shape(4, 16, 2 * FF + 128)] * 4,
        [where, half, other, norm_gain.reshape(1, 448), gate_weight, up_weight],
        scalars=1,
        limit=30,
    )
    got = [sums[0]] + [send_dp(sums[k], 0, k) for k in (2, 1, 3)]
    sums = call(fold_kernel, "fold", [shape(16, 2 * FF + 128)] * 4, got)
    got = [sums[0]] + [send_dp(sums[k], 1, k) for k in (2, 1, 3)]
    (hidden,) = call(finish_kernel, "finish", [shape(16, FF)], got)
    return (turn(stream.reshape(256, 448)).T, hidden)


def solution(mesh):
    placed = (
        P("dp", "tp"),
        P("dp", None),
        P(("dp", "tp"), None),
        P(),
        P(),
        P(),
        P("tp", None, None),
        P("tp", "dp"),
        P(None, "dp"),
        P("dp"),
        P("dp", "tp"),
        P("dp", "tp"),
    )
    return jax.shard_map(
        local, mesh=mesh, in_specs=placed, out_specs=(P(None, "dp"), P("dp", "tp")), check_vma=False
    )
```

```python
import functools
import math

import jax
import jax.numpy as jnp
from jax import lax
from jax.experimental import pallas as pl
from jax.experimental.pallas import tpu as pltpu
from jax.sharding import PartitionSpec as P

D = 7168
LAT = 512
ROPE = 64
QK_NOPE = 128
CAP = 2
PB = 512
BS = 64
KV = LAT + ROPE
EPSILON = 1e-06
FF = 2304
SCALE = 1.0 / math.sqrt(QK_NOPE + ROPE)
SCALE2 = SCALE / math.log(2.0)
NEG = -1e30
f32 = jnp.float32
bf16 = jnp.bfloat16


def send(x, axis, to, n):
    return lax.ppermute(x, axis, [(i, to(i)) for i in range(n)])


def swap_core(x):
    return send(x, "tp", lambda i: i ^ 1, 8)


def send_y(x, k):
    return send(x, "tp", lambda i: i ^ (2 * k), 8)


def send_dp(x, stage, k):
    pairs = []
    for i in range(128):
        dp, tp = i // 8, i % 8
        if tp % 2 == stage:
            to = ((dp // 4 + k) % 4) * 4 + dp % 4
        else:
            to = (dp // 4) * 4 + (dp % 4 + k) % 4
        pairs.append((i, to * 8 + tp))
    return lax.ppermute(x, ("dp", "tp"), pairs)


VMEM = pl.BlockSpec(memory_space=pltpu.VMEM)
SMEM = pl.BlockSpec(memory_space=pltpu.SMEM)
ANY = pl.BlockSpec(memory_space=pl.ANY)


def call(kernel, name, outs, ins, scalars=0, anys=0, limit=20, **kw):
    return pl.pallas_call(
        kernel,
        out_shape=outs,
        in_specs=[SMEM] * scalars + [VMEM] * (len(ins) - scalars - anys) + [ANY] * anys,
        out_specs=[VMEM] * len(outs),
        compiler_params=pltpu.CompilerParams(vmem_limit_bytes=limit * 1024 * 1024),
        name=name,
        **kw,
    )(*ins)


def shape(*dims, dtype=bf16):
    return jax.ShapeDtypeStruct(dims, dtype)


def place_of(where, ka, kb):
    px, pz, core = where[0], where[1], where[2]
    kx = jnp.where(core == 0, ka, kb)
    kz = jnp.where(core == 0, kb, ka)
    return ((px + kx) % 4) * 4 + (pz + kz) % 4


def plan_kernel(where, home_ref, prompt_ref, chosen_ref, picks_ref):
    px, pz, lane = where[0], where[1], where[3]
    replica = px * 4 + pz
    i32 = jnp.int32
    home = home_ref[...].reshape(16, 128)
    ids = lax.broadcasted_iota(i32, (16, 128), 0) * 128 + lax.broadcasted_iota(i32, (16, 128), 1)
    chosen = chosen_ref[...]
    wanted = chosen + prompt_ref[...] * PB
    asked = []
    for slot in range(16):
        found = home == (replica * 8 + lane) * 16 + slot
        block = jnp.sum(jnp.where(found, ids, 0), axis=(0, 1), keepdims=True)
        asked.append(jnp.max(jnp.where(wanted == block, 1.0, 0.0), axis=0, keepdims=True))
    asked = jnp.concatenate(asked, axis=0).astype(bf16)
    row = lax.broadcasted_iota(i32, (256, 128), 0)
    owner = lax.broadcasted_iota(i32, (256, 128), 1)
    owns = jnp.where(row // 16 == owner, 1.0, 0.0).astype(bf16)
    needed = jnp.dot(asked, owns, preferred_element_type=f32) > 0.5
    flag = jnp.where(needed, 1.0, 0.0)
    slot = lax.broadcasted_iota(i32, (16, 128), 0)
    low = lax.broadcasted_iota(i32, (16, 16), 0) > lax.broadcasted_iota(i32, (16, 16), 1)
    low = jnp.where(low, 1.0, 0.0).astype(bf16)
    before = jnp.dot(low, flag.astype(bf16), preferred_element_type=f32)
    for rank in range(CAP):
        pick = needed & (before > rank - 0.5) & (before < rank + 0.5)
        picks_ref[rank : rank + 1] = jnp.sum(jnp.where(pick, slot, 0), axis=0, keepdims=True)


def use_kernel(where, prompts, home_ref, chosen_ref, _, use_ref):
    px, pz, core, lane = where[0], where[1], where[2], where[3]
    replica = px * 4 + pz
    i32 = jnp.int32
    chosen = chosen_ref[...]
    mine = pltpu.roll(chosen, (256 - replica * 16) % 256, 1)[:, :128]
    mine = jnp.concatenate([mine.astype(f32), jnp.zeros((96, 128), f32)], axis=0).T[:16]
    block = lax.broadcasted_iota(i32, (16, PB), 1).astype(f32)
    uses = jnp.zeros((16, PB), f32)
    for t in range(32):
        uses = jnp.where(mine[:, t : t + 1] == block, 1.0, uses)
    need = jnp.max(uses, axis=0, keepdims=True) > 0.5
    here = home_ref[prompts[replica * 16]]
    here = jnp.concatenate([here[i : i + 1] for i in range(4)], axis=1)
    holder = here // 16
    live = jnp.where(need, here, -1).astype(f32)
    column = jnp.broadcast_to(live, (128, PB)).T[:, :1].astype(i32)
    fewer = (column // 16 == holder) & (column < here) & (column >= 0)
    rank = jnp.sum(jnp.where(fewer, 1, 0), axis=0, keepdims=True)
    key = jnp.where(need, holder * CAP + rank, -1)
    at = lax.broadcasted_iota(i32, (64, PB), 0)
    piece, ka, place = at // 8, (at // 2) % 4, at % 2
    sib = jnp.where((piece == 1) | (piece >= 5), 1, 0)
    kb = jnp.where(piece < 2, 0, (piece + 1) % 3 + 1)
    from_core = core ^ sib
    kx = jnp.where(from_core == 0, ka, kb)
    kz = jnp.where(from_core == 0, kb, ka)
    dev = (((px + 4 - kx) % 4) * 4 + (pz + 4 - kz) % 4) * 8 + lane - core + from_core
    hit = jnp.where(dev * CAP + place == key, 1.0, 0.0).astype(bf16)
    use = lax.dot_general(
        uses.astype(bf16), hit, (((1,), (1,)), ((), ())), preferred_element_type=f32
    )
    use_ref[...] = use.astype(bf16)


def fetch_kernel(where, picks, tokens, *outs):
    for ka in range(4):
        for kb in range(4):
            dest = place_of(where, ka, kb)
            for rank in range(CAP):
                pick = picks[rank, dest]
                out = outs[ka]
                at = kb * CAP + rank
                for c in range(4):
                    out[at, c * BS : (c + 1) * BS, :] = tokens[pick, :, c * 128 : (c + 1) * 128]
                rope = tokens[pick, :, LAT:KV]
                out[at, 4 * BS :, :] = jnp.concatenate([rope[:32], rope[32:]], axis=1)


def ask_kernel(queries, own, _, q_ref, own_ref):
    for head in range(16):
        x = queries[:, head * KV : (head + 1) * KV]
        rows = slice(head * 16, (head + 1) * 16)
        q_ref[rows, :LAT] = x[:, :LAT]
        q_ref[rows, LAT:] = jnp.concatenate([x[:, LAT:], x[:, LAT:]], axis=1)
    x = own[...]
    own_ref[:, :LAT] = x[:, :LAT]
    own_ref[:, LAT:] = jnp.concatenate([x[:, LAT:], x[:, LAT:]], axis=1)


def regroup_kernel(*refs):
    refs = refs[:4] + refs[6:]
    for ka in range(4):
        for kb in range(4):
            refs[4 + kb][ka * CAP : (ka + 1) * CAP] = refs[ka][kb * CAP : (kb + 1) * CAP]


def after_kernel(_, *refs):
    count = len(refs) // 2
    for i in range(count):
        refs[count + i][...] = refs[i][...]


def after(first, *blocks):
    return call(after_kernel, "after", [shape(8, 288, 128)] * len(blocks), [first, *blocks])


def half_latent(refs, half):
    rows = []
    for ref in refs:
        parts = [
            ref[:, c * BS + half * 32 : c * BS + half * 32 + 32, :].reshape(-1, 128)
            for c in range(4)
        ]
        rows.append(jnp.concatenate(parts, axis=1))
    return jnp.concatenate(rows, axis=0)


def half_rope(refs, half):
    rope = jnp.concatenate(
        [ref[:, 4 * BS : 4 * BS + 32, :].reshape(-1, 128) for ref in refs], axis=0
    )
    lane = lax.broadcasted_iota(jnp.int32, rope.shape, 1)
    keep = (lane < ROPE) if half == 0 else (lane >= ROPE)
    return jnp.where(keep, rope, jnp.zeros_like(rope))


def attend_kernel(first, sizes, chips, resume, last, *refs):
    groups, count = len(sizes), sum(sizes)
    use_ref, refs = refs[0], refs[1:]
    qs, refs = dict(zip(chips, refs)), refs[len(chips) :]
    pieces, refs = refs[:count], refs[count:]
    if resume:
        (acc_in, stat_in), refs = refs[:2], refs[2:]
    m_rows = 256
    members, biases = [], []
    for g, size in enumerate(sizes):
        at = sum(sizes[:g])
        members.append(pieces[at : at + size])
        slot = lax.broadcasted_iota(jnp.int32, (64, size * 512), 0)
        token = lax.broadcasted_iota(jnp.int32, (64, size * 512), 1)
        spread = (token // 32) % (8 * size) + 8 * (first + at) == slot
        spread = spread.astype(f32).astype(bf16)
        used = jnp.dot(use_ref[...], spread, preferred_element_type=f32)
        biases.append((used - 1.0) * -NEG)

    def values(g):
        return jnp.concatenate([half_latent(members[g], h) for h in range(2)], axis=0)

    def scores(chip, g):
        ropes = jnp.concatenate([half_rope(members[g], h) for h in range(2)], axis=0)
        keys = jnp.concatenate([values(g), ropes], axis=1)
        s = lax.dot_general(
            qs[chip][...], keys, (((1,), (1,)), ((), ())), preferred_element_type=f32
        )
        n = s.shape[1]
        return (s.reshape(m_rows // 16, 16, n) + biases[g][None]).reshape(m_rows, n)

    steps = [(chip, g) for chip in chips for g in range(groups)]
    s = scores(*steps[0])
    for i, (chip, g) in enumerate(steps):
        ahead = scores(*steps[i + 1]) if i + 1 < len(steps) else None
        if g == 0:
            top = total = acc = None
            if resume:
                top, total = stat_in[chip, :, 0:1], stat_in[chip, :, 64:65]
                acc = acc_in[chip]
        high = jnp.max(s, axis=1, keepdims=True)
        new = high if top is None else jnp.maximum(top, high)
        p = jnp.exp2((s - new) * SCALE2)
        part = jnp.sum(p, axis=1, keepdims=True)
        o = jnp.dot(p.astype(bf16), values(g), preferred_element_type=f32)
        if top is None:
            acc, total = o, part
        else:
            fade = jnp.exp2((top - new) * SCALE2)
            acc, total = acc * fade + o, total * fade + part
        top, s = new, ahead
        if g == groups - 1 and last:
            finish_heads(acc, top, total, refs[chips.index(chip)])
        elif g == groups - 1:
            lane = lax.broadcasted_iota(jnp.int32, (m_rows, 128), 1)
            refs[0][chip] = acc
            refs[1][chip] = jnp.where(lane < 64, top, total)
    if not last:
        refs[2][...] = jnp.zeros((8, 128), f32)


def finish_heads(acc, top, total, out_ref):
    m_rows = 256
    out_ref[:m_rows] = (acc / total).astype(bf16)
    lse = top * SCALE + jnp.log(total)
    hi = lse.astype(bf16).astype(f32)
    mid = (lse - hi).astype(bf16).astype(f32)
    low = lse - hi - mid
    lane = lax.broadcasted_iota(jnp.int32, (m_rows, 128), 1)
    stats = jnp.where(lane == 0, hi, jnp.where(lane == 1, mid, jnp.where(lane == 2, low, 0.0)))
    stats = stats.T[:16]
    out_ref[m_rows:] = jnp.concatenate([stats, jnp.zeros_like(stats)], axis=1).astype(bf16)


def attend(use, qs, first, sizes, pieces, carry=(), last=True):
    if last:
        outs = [shape(256 + 16, LAT)] * len(qs)
    else:
        outs = [shape(4, 256, LAT, dtype=f32), shape(4, 256, 128, dtype=f32)]
        outs.append(shape(8, 128, dtype=f32))
    return call(
        functools.partial(attend_kernel, first, sizes, list(qs), bool(carry), last),
        "attend",
        outs,
        [use, *qs.values(), *pieces, *carry],
        limit=16,
    )


def merge_kernel(o0, o1, o2, o3, q_ref, own_ref, up_ref, out_ref):
    heads, rows = 16, 16
    own = own_ref[...].astype(f32)
    q = q_ref[...].astype(f32).reshape(heads, rows, 640)
    lane = lax.broadcasted_iota(jnp.int32, (rows, 640), 1)
    key = jnp.where(lane < KV, own, 0.0)
    s_own = jnp.sum(q * key[None], axis=2, keepdims=True).reshape(heads * rows, 1) * SCALE
    lses = []
    for o in (o0, o1, o2, o3):
        row = jnp.sum(o[256:, :256].astype(f32), axis=0, keepdims=True)
        lses.append(jnp.broadcast_to(row, (128, 256)).T[:, :1])
    top = s_own
    for v in lses:
        top = jnp.maximum(top, v)
    e_own = jnp.exp(s_own - top)
    es = [jnp.exp(v - top) for v in lses]
    den = e_own + ((es[0] + es[1]) + (es[2] + es[3]))
    mix = (e_own / den).reshape(heads, rows, 1) * own[None, :, :LAT]
    mix = mix.reshape(heads * rows, LAT)
    for o, e in zip((o0, o1, o2, o3), es):
        mix = mix + (e / den) * o[:256].astype(f32)
    mix = mix.astype(bf16)
    for h in range(heads):
        out_ref[:, h * 128 : (h + 1) * 128] = jnp.dot(
            mix[h * rows : (h + 1) * rows], up_ref[h], preferred_element_type=f32
        ).astype(bf16)


def merge(parts, q, own, value_up):
    return pl.pallas_call(
        merge_kernel,
        out_shape=jax.ShapeDtypeStruct((16, 2048), bf16),
        in_specs=[pl.BlockSpec(memory_space=pltpu.VMEM)] * 7,
        out_specs=pl.BlockSpec(memory_space=pltpu.VMEM),
        compiler_params=pltpu.CompilerParams(vmem_limit_bytes=24 * 1024 * 1024),
        name="merge",
    )(*parts, q, own, value_up)


def project_kernel(where, p0, p1, p2, p3, weight, keep_ref, give_ref):
    core = where[2]
    rows = jnp.concatenate([p0[...], p1[...], p2[...], p3[...]], axis=0)
    full = lax.dot_general(
        rows, weight[...], (((1,), (1,)), ((), ())), preferred_element_type=f32
    ).reshape(4, 4, 16, 448)

    @pl.when(core == 0)
    def _():
        keep_ref[...] = full[:2]
        give_ref[...] = full[2:].astype(bf16)

    @pl.when(core == 1)
    def _():
        for i in range(2):
            keep_ref[i] = full[:, 2 + i]
            give_ref[i] = full[:, i].astype(bf16)


def join_kernel(where, pair, t1, t2, t3, residual, out):
    px, pz, core = where[0], where[1], where[2]
    for i in range(2):
        for kx in range(4):
            kz = core * 2 + i
            dp = ((px + kx) % 4) * 4 + (pz + kz) % 4
            attn = (pair[i, kx].astype(f32) + t1[i, kx].astype(f32)) + (
                t2[i, kx].astype(f32) + t3[i, kx].astype(f32)
            )
            out[i, kx] = (residual[dp].astype(f32) + attn).astype(bf16)


def ffn_kernel(where, half_ref, other_ref, gain_ref, wg_ref, wu_ref, stream_ref, *outs):
    px, pz, core = where[0], where[1], where[2]
    half, other = half_ref[...].astype(f32), other_ref[...].astype(f32)
    rows = jnp.concatenate(
        [jnp.where(core == 0, half, other), jnp.where(core == 0, other, half)], axis=0
    )
    for kz in range(4):
        for kx in range(4):
            stream_ref[((px + kx) % 4) * 4 + (pz + kz) % 4] = rows[kz, kx].astype(bf16)
    turned = jnp.stack([rows[:, k] for k in range(4)], axis=0)
    wide = jnp.where(core == 0, rows, turned).reshape(256, 448)
    squares = jnp.sum(wide * wide, axis=1, keepdims=True)
    hi = squares.astype(bf16).astype(f32)
    lane = lax.broadcasted_iota(jnp.int32, (256, 128), 1)
    tail = jnp.where(lane == 0, hi, jnp.where(lane == 1, squares - hi, 0.0)).astype(bf16)
    scaled = (wide * gain_ref[...].astype(f32)).astype(bf16)
    gate = jnp.dot(scaled, wg_ref[...], preferred_element_type=f32).astype(bf16)
    gate = gate.reshape(4, 4, 16, FF)
    tail = tail.reshape(4, 4, 16, 128)
    for k in range(4):
        outs[k][:, :, :FF] = gate[:, k]
        outs[k][:, :, 2 * FF :] = tail[:, k]
    up = jnp.dot(scaled, wu_ref[...], preferred_element_type=f32).astype(bf16)
    up = up.reshape(4, 4, 16, FF)
    for k in range(4):
        outs[k][:, :, FF : 2 * FF] = up[:, k]


def turn_kernel(x, out):
    out[...] = x[...].astype(f32).T.astype(bf16)


def turn(x):
    return call(turn_kernel, "turn", [shape(x.shape[1], x.shape[0])], [x])[0]


def sum4(refs, at):
    a, b, c, d = (ref[at].astype(f32) for ref in refs)
    return (a + b) + (c + d)


def fold_kernel(*refs):
    for kb in range(4):
        s = sum4(refs[:4], kb)
        refs[4 + kb][:, : 2 * FF] = s[:, : 2 * FF].astype(bf16)
        squares = jnp.sum(s[:, 2 * FF :], axis=1, keepdims=True)
        hi = squares.astype(bf16).astype(f32)
        lane = lax.broadcasted_iota(jnp.int32, (16, 128), 1)
        tail = jnp.where(lane == 0, hi, jnp.where(lane == 1, squares - hi, 0.0))
        refs[4 + kb][:, 2 * FF :] = tail.astype(bf16)


def finish_kernel(r0, r1, r2, r3, out):
    s = sum4((r0, r1, r2, r3), ...)
    squares = jnp.sum(s[:, 2 * FF :], axis=1, keepdims=True)
    inverse = lax.rsqrt(squares / D + EPSILON)
    gate = s[:, :FF] * inverse
    up = s[:, FF : 2 * FF] * inverse
    out[...] = (gate / (1.0 + jnp.exp(-gate)) * up).astype(bf16)


def local(
    queries,
    own_latent,
    prefix_cache,
    block_home,
    row_prompt,
    chosen,
    value_up,
    out_weight,
    residual,
    norm_gain,
    gate_weight,
    up_weight,
):
    replica = lax.axis_index("dp")
    lane = lax.axis_index("tp")
    px, pz = replica // 4, replica % 4
    core = lane % 2
    i32 = jnp.int32
    where = jnp.stack([px, pz, core, lane]).astype(i32)

    homes = block_home.reshape(4, 4, 128)
    (picks,) = call(
        plan_kernel,
        "plan",
        [shape(CAP, 128, dtype=i32)],
        [where, homes, row_prompt.reshape(1, 256), chosen.T],
        scalars=1,
    )

    sent = call(
        fetch_kernel,
        "fetch",
        [shape(8, 288, 128)] * 4,
        [where, picks, prefix_cache.reshape(16, BS, KV)],
        scalars=2,
    )
    got = [sent[0]] + [send_dp(sent[k], 0, k) for k in (1, 2, 3)]

    (use,) = call(
        use_kernel,
        "use",
        [shape(16, 64)],
        [where, row_prompt, homes, chosen.T, sent[0]],
        scalars=2,
        anys=1,
    )

    q, own = call(
        ask_kernel,
        "ask",
        [shape(256, LAT + 128), shape(16, LAT + 128)],
        [queries, own_latent, sent[0]],
        anys=1,
    )
    qs = {0: q, **{k: send_y(q, k) for k in (1, 2, 3)}}

    groups = call(regroup_kernel, "regroup", [shape(8, 288, 128)] * 4, [*got, use, qs[2]], anys=2)
    arrived = {0: groups[0]}
    for k in (1, 3, 2):
        arrived[k] = send_dp(groups[k], 1, k)
    pieces = [groups[0], swap_core(groups[0])]
    *carry, done = attend(use, qs, 0, (2,), pieces, last=False)
    far = after(done, arrived[1], arrived[2], arrived[3])
    far_other = [swap_core(v) for v in far]
    others = {k: qs[k] for k in (2, 1, 3)}
    *rest, done = attend(use, others, 2, (3,), far, carry, last=False)
    parts = []
    for k in others:
        (o,) = attend(use, {k: qs[k]}, 5, (3,), far_other, rest)
        parts.append(send_y(o, k))
    parts += attend(use, {0: q}, 2, (3, 3), list(far) + far_other, carry)
    per_head = merge(parts, q, own, value_up)

    near = [per_head] + [send_dp(per_head, 0, 4 - k) for k in (1, 2, 3)]
    near = jnp.concatenate(near, axis=0)
    far = [near] + [send_dp(near, 1, 4 - k) for k in (1, 2, 3)]
    keep, give = call(
        project_kernel,
        "project",
        [shape(2, 4, 16, 448, dtype=f32), shape(2, 4, 16, 448)],
        [where, *far, out_weight.T],
        scalars=1,
    )
    pair = (keep + swap_core(give).astype(f32)).astype(bf16)
    terms = [send_y(pair, k) for k in (1, 2, 3)]
    (half,) = call(
        join_kernel,
        "join",
        [shape(2, 4, 16, 448)],
        [where, pair, *terms, turn(residual.T).reshape(16, 16, 448)],
        scalars=1,
    )
    other = swap_core(half)
    stream, *sums = call(
        ffn_kernel,
        "ffn",
        [shape(16, 16, 448)] + [shape(4, 16, 2 * FF + 128)] * 4,
        [where, half, other, norm_gain.reshape(1, 448), gate_weight, up_weight],
        scalars=1,
        limit=30,
    )
    got = [sums[0]] + [send_dp(sums[k], 0, k) for k in (2, 1, 3)]
    sums = call(fold_kernel, "fold", [shape(16, 2 * FF + 128)] * 4, got)
    got = [sums[0]] + [send_dp(sums[k], 1, k) for k in (2, 1, 3)]
    (hidden,) = call(finish_kernel, "finish", [shape(16, FF)], got)
    return (turn(stream.reshape(256, 448)).T, hidden)


def solution(mesh):
    placed = (
        P("dp", "tp"),
        P("dp", None),
        P(("dp", "tp"), None),
        P(),
        P(),
        P(),
        P("tp", None, None),
        P("tp", "dp"),
        P(None, "dp"),
        P("dp"),
        P("dp", "tp"),
        P("dp", "tp"),
    )
    return jax.shard_map(
        local, mesh=mesh, in_specs=placed, out_specs=(P(None, "dp"), P("dp", "tp")), check_vma=False
    )
```
